128 devices in a mesh: seq: 32 (over z, x, core), head: 4 (over y).
Axes of the slice: x: 4, y: 4, z: 4, core: 2. Of those that a mesh axis runs over, the one named last changes fastest.
Arguments:
- queries: bfloat16 [32768, 4096], P('seq', 'head'), may hold values from -6 to 6
- keys: bfloat16 [32768, 4096], P('seq', 'head'), may hold values from -6 to 6
- values: bfloat16 [32768, 4096], P('seq', 'head'), may hold values from -6 to 6
- out_weight: bfloat16 [4096, 4096], P('head', 'seq'), may hold values from -0.09375 to 0.09375
Outputs:
- mixed: bfloat16 [32768, 4096], P('seq', 'head')
The draws below stay inside these ranges and needn't reach their ends.
All inputs are finite; a program needn't handle non-finite values.
Results may differ from the reference program's by a relative error of at most 0.015.
Values may be sent and summed in bfloat16 or wider, within the bound.
No kernel may reach another device: no remote copies, remote signals or barrier semaphores. Data moves between devices by JAX's collectives and lax.ppermute only.
A program may use at most 128 MiB of HBM per device.

```python
import jax
import jax.numpy as jnp
from jax import lax

D = 4096
HEADS = 32
HEAD_DIM = 128
BLOCK = 512
TOKENS = 32768
FEATURES = 4096
N_HEAD = 4


def block_levels(stream_key, dims, split, least, largest):
    loudness = 1.0
    for dim, shards_of in split:
        steps = jax.random.uniform(jax.random.fold_in(jax.random.fold_in(stream_key, 6), dim), (shards_of,), jnp.float32, least / len(split), largest / len(split))
        loudness = loudness * jnp.repeat(jnp.exp(steps), dims[dim] // shards_of).reshape((-1,) + (1,) * (len(dims) - 1 - dim))
    return loudness


def noise(rng, shape, width, most, cuts=(), dtype=jnp.bfloat16):
    level = block_levels(rng, shape, cuts, -0.22, 0.18) if cuts else 1.0
    drawn = jax.random.normal(rng, shape, jnp.float32) * width * level
    return jnp.minimum(jnp.maximum(drawn, -most), most).astype(dtype)


def setup_inputs(seed: int = 0) -> dict:
    arg_keys = jax.random.split(jax.random.key(seed), 5)
    return {
        "queries": noise(arg_keys[0], (TOKENS, FEATURES), 1.0, 6.0, ((0, 32), (1, 4))),
        "keys": noise(arg_keys[1], (TOKENS, FEATURES), 1.0, 6.0, ((0, 32), (1, 4))),
        "values": noise(arg_keys[2], (TOKENS, FEATURES), 1.0, 6.0, ((0, 32), (1, 4))),
        "out_weight": noise(arg_keys[3], (FEATURES, D), FEATURES ** -0.5, 0.09375, ((0, 4), (1, 32))),
    }


EPSILON = 1e-06

def feature(source):
    return (jax.nn.elu(source.astype(jnp.float32)) + 1.0).astype(jnp.bfloat16)

def reference(queries, keys, values, out_weight):
    groups = N_HEAD
    features = HEADS * HEAD_DIM
    nblocks = TOKENS // BLOCK

    def blockwise(source):
        return source.reshape(nblocks, BLOCK, HEADS, HEAD_DIM)
    query_blocks = blockwise(queries)
    key_blocks = blockwise(keys)
    value_blocks = blockwise(values)
    weight = out_weight.astype(jnp.float32).reshape(groups, features // groups, D)
    causal = jnp.tril(jnp.ones((BLOCK, BLOCK), jnp.bool_))

    def advance(running, blocks_now):
        query_now, key_now, value_now = blocks_now
        query_feat = feature(query_now).astype(jnp.float32)
        key_feat = feature(key_now).astype(jnp.float32)
        value_rows = value_now.astype(jnp.float32)
        scores = jnp.einsum('thd,shd->hts', query_feat, key_feat)
        scores = jnp.where(causal[None], scores, 0.0).astype(jnp.bfloat16)
        scores = lax.optimization_barrier(scores).astype(jnp.float32)
        local_part = jnp.einsum('hts,she->the', scores, value_rows)
        start_state = lax.optimization_barrier(running.astype(jnp.bfloat16)).astype(jnp.float32)
        carried_part = jnp.einsum('thd,hde->the', query_feat, start_state)
        combined = local_part + carried_part
        scale = lax.rsqrt(lax.optimization_barrier(jnp.mean(combined * combined, axis=-1, keepdims=True)) + EPSILON)
        normed = (combined * scale).astype(jnp.bfloat16).astype(jnp.float32)
        normed = normed.reshape(BLOCK, groups, features // groups)
        group_parts = jnp.einsum('tgf,gfe->gte', normed, weight)
        group_parts = lax.optimization_barrier(group_parts.astype(jnp.bfloat16)).astype(jnp.float32)
        mixed_block = lax.optimization_barrier(jnp.sum(group_parts, axis=0)).astype(jnp.bfloat16)
        updated = running + jnp.einsum('thd,the->hde', key_feat, value_rows)
        return (updated, mixed_block)
    initial = jnp.zeros((HEADS, HEAD_DIM, HEAD_DIM), jnp.float32)
    _, outputs = lax.scan(advance, initial, (query_blocks, key_blocks, value_blocks))
    return outputs.reshape(TOKENS, D)
```

```python
import functools

import jax
import jax.numpy as jnp
from jax import lax
from jax.experimental import pallas as pl
from jax.experimental.pallas import tpu as pltpu
from jax.sharding import PartitionSpec as P

HEAD_DIM = 128
BLOCK = 512
EPSILON = 1e-06
AXES = ("seq", "head")
NZ, NX, NC, NY = 4, 4, 2, 4
OFFSETS = (0, 1, -1, 2)
QROWS = 256
CHUNKS = ((0, 128), (128, 128), (256, 256), (512, 256), (768, 128), (896, 128))
VMEM_LIMIT = 48 * 1024 * 1024


def route(target):
    pairs = []
    for z in range(NZ):
        for x in range(NX):
            for c in range(NC):
                for y in range(NY):
                    z2, x2, c2, y2 = target(z, x, c, y)
                    source = ((z * NX + x) * NC + c) * NY + y
                    to = (((z2 % NZ) * NX + x2 % NX) * NC + c2) * NY + y2
                    pairs.append((source, to))
    return pairs


def send(array, target):
    return lax.ppermute(array, AXES, route(target))


def params():
    return pltpu.CompilerParams(vmem_limit_bytes=VMEM_LIMIT)


def feature(source):
    wide = source.astype(jnp.float32)
    return jnp.where(wide > 0, wide + 1.0, jnp.exp(jnp.minimum(wide, 0.0))).astype(jnp.bfloat16)


def state_kernel(keys_ref, values_ref, feat_ref, total_ref, first_ref):
    for head in range(keys_ref.shape[1] // HEAD_DIM):
        columns = slice(head * HEAD_DIM, (head + 1) * HEAD_DIM)
        feat = feature(keys_ref[:, columns])
        feat_ref[:, columns] = feat
        sums = []
        for block in range(2):
            rows = slice(block * BLOCK, (block + 1) * BLOCK)
            sums.append(
                lax.dot_general(
                    feat[rows],
                    values_ref[rows, columns],
                    (((0,), (0,)), ((), ())),
                    preferred_element_type=jnp.float32,
                )
            )
        first_ref[head] = sums[0]
        total_ref[head] = (sums[0] + sums[1]).astype(jnp.bfloat16)


def states(keys, values):
    tokens, features = keys.shape
    heads = features // HEAD_DIM
    step = 2
    wide = pl.BlockSpec((tokens, step * HEAD_DIM), lambda i: (0, i))
    square = pl.BlockSpec((step, HEAD_DIM, HEAD_DIM), lambda i: (i, 0, 0))
    return pl.pallas_call(
        state_kernel,
        grid=(heads // step,),
        in_specs=[wide, wide],
        out_specs=[wide, square, square],
        out_shape=[
            jax.ShapeDtypeStruct((tokens, features), jnp.bfloat16),
            jax.ShapeDtypeStruct((heads, HEAD_DIM, HEAD_DIM), jnp.bfloat16),
            jax.ShapeDtypeStruct((heads, HEAD_DIM, HEAD_DIM), jnp.float32),
        ],
        compiler_params=params(),
        cost_estimate=pl.CostEstimate(
            flops=2 * tokens * features * HEAD_DIM,
            bytes_accessed=6 * tokens * features,
            transcendentals=tokens * features,
        ),
        name="states",
    )(keys, values)


def local_kernel(queries_ref, feat_ref, values_ref, local_ref, query_feat_ref):
    rows = queries_ref.shape[0]
    span = feat_ref.shape[0]
    row = lax.broadcasted_iota(jnp.int32, (rows, rows), 0)
    column = lax.broadcasted_iota(jnp.int32, (rows, rows), 1)
    causal = column <= row
    for head in range(queries_ref.shape[1] // HEAD_DIM):
        columns = slice(head * HEAD_DIM, (head + 1) * HEAD_DIM)
        query_feat = feature(queries_ref[:, columns])
        query_feat_ref[:, columns] = query_feat
        scores = lax.dot_general(
            query_feat,
            feat_ref[:, columns],
            (((1,), (1,)), ((), ())),
            preferred_element_type=jnp.float32,
        )
        diagonal = jnp.where(causal, scores[:, span - rows :], 0.0).astype(jnp.bfloat16)
        out = jnp.dot(
            diagonal, values_ref[span - rows :, columns], preferred_element_type=jnp.float32
        )
        if span > rows:
            out += jnp.dot(
                scores[:, : span - rows].astype(jnp.bfloat16),
                values_ref[: span - rows, columns],
                preferred_element_type=jnp.float32,
            )
        local_ref[:, columns] = out


def local_part(queries, key_feat, values, index):
    features = queries.shape[1]
    width = features // 2
    span = QROWS * (index % 2 + 1)
    first = (index // 2) * (BLOCK // span)
    rows = pl.BlockSpec((QROWS, width), lambda i: (index, i))
    source = pl.BlockSpec((span, width), lambda i: (first, i))
    out = pl.BlockSpec((QROWS, width), lambda i: (0, i))
    return pl.pallas_call(
        local_kernel,
        grid=(features // width,),
        in_specs=[rows, source, source],
        out_specs=[out, out],
        out_shape=[
            jax.ShapeDtypeStruct((QROWS, features), jnp.float32),
            jax.ShapeDtypeStruct((QROWS, features), jnp.bfloat16),
        ],
        compiler_params=params(),
        cost_estimate=pl.CostEstimate(
            flops=4 * QROWS * span * features,
            bytes_accessed=(8 * QROWS + 4 * span) * features,
            transcendentals=QROWS * features,
        ),
        name="local_part",
    )(queries, key_feat, values)


def norm_kernel(local_ref, query_feat_ref, start_ref, normed_ref):
    for head in range(local_ref.shape[1] // HEAD_DIM):
        columns = slice(head * HEAD_DIM, (head + 1) * HEAD_DIM)
        combined = local_ref[:, columns] + jnp.dot(
            query_feat_ref[:, columns], start_ref[0, head], preferred_element_type=jnp.float32
        )
        mean = jnp.mean(combined * combined, axis=-1, keepdims=True)
        normed_ref[:, columns] = (combined * lax.rsqrt(mean + EPSILON)).astype(jnp.bfloat16)


def norm_part(local, query_feat, start, row, rows):
    features = local.shape[1]
    heads = features // HEAD_DIM
    block = row // BLOCK
    place = (row % QROWS) // rows
    spec = pl.BlockSpec((rows, features), lambda i: (place, 0))
    return pl.pallas_call(
        norm_kernel,
        grid=(1,),
        in_specs=[
            spec,
            spec,
            pl.BlockSpec((1, heads, HEAD_DIM, HEAD_DIM), lambda i: (block, 0, 0, 0)),
        ],
        out_specs=pl.BlockSpec((rows, features), lambda i: (0, 0)),
        out_shape=jax.ShapeDtypeStruct((rows, features), jnp.bfloat16),
        compiler_params=params(),
        cost_estimate=pl.CostEstimate(
            flops=2 * rows * features * HEAD_DIM,
            bytes_accessed=8 * rows * features + 2 * features * HEAD_DIM,
            transcendentals=rows * heads,
        ),
        name="norm_part",
    )(local, query_feat, start)


def position():
    seq = lax.axis_index("seq")
    return seq // (NX * NC), (seq // NC) % NX, seq % NC, lax.axis_index("head")


def project_kernel(own_columns, has_sum, *refs):
    normed_ref, peer_ref = refs[:2]
    pieces = refs[2:10]
    received_ref = refs[10] if has_sum else None
    out_ref, weight, arrived = refs[-3:]
    z, x, c, y = position()
    rows = weight.shape[1] // NC
    width = weight.shape[2] // NX
    for index, piece in enumerate(pieces):
        away = OFFSETS[index % 4]
        core = c if index < 4 else 1 - c
        for inner, near in enumerate(OFFSETS):
            from_z = lax.rem(z + jnp.where(core == 0, away, near) + NZ, NZ)
            from_x = lax.rem(x + jnp.where(core == 0, near, away) + NX, NX)
            kind = jnp.bitwise_xor(from_z, y)
            slot = kind if own_columns else 3 - kind

            @pl.when((slot >= 0) & (slot < 2))
            def _():
                pltpu.make_async_copy(
                    piece.at[inner],
                    weight.at[
                        slot,
                        pl.ds(pl.multiple_of(core * rows, rows), rows),
                        pl.ds(pl.multiple_of(from_x * width, width), width),
                    ],
                    arrived.at[from_x],
                ).start()

    for tile in range(NX):
        columns = slice(tile * width, (tile + 1) * width)
        for _ in range(4):
            pltpu.make_async_copy(
                pieces[0].at[0], weight.at[0, pl.ds(0, rows), columns], arrived.at[tile]
            ).wait()
        total = jnp.dot(
            normed_ref[...], weight[0, :, columns], preferred_element_type=jnp.float32
        )
        total += jnp.dot(peer_ref[...], weight[1, :, columns], preferred_element_type=jnp.float32)
        if has_sum:
            total += received_ref[:, columns].astype(jnp.float32)
        out_ref[:, columns] = total.astype(jnp.bfloat16)


def project(normed, peer, pieces, received=None, row=0, tokens=0, target=None):
    rows, features = normed.shape
    own = received is not None
    chunk = pl.BlockSpec((rows, features), lambda i: (0, 0))
    place = row // rows if own else 0
    operands = [normed, peer, *pieces]
    specs = [chunk, chunk] + [pl.BlockSpec(memory_space=pl.ANY)] * len(pieces)
    aliases = {}
    if own:
        operands.append(received)
        specs.append(chunk)
        if target is not None:
            aliases = {len(operands): 0}
            operands.append(target)
            specs.append(pl.BlockSpec(memory_space=pl.ANY))

    def body(*refs):
        refs = list(refs)
        if target is not None:
            del refs[11]
        project_kernel(own, own, *refs)

    return pl.pallas_call(
        body,
        grid=(1,),
        in_specs=specs,
        out_specs=pl.BlockSpec((rows, features), lambda i: (place, 0)),
        out_shape=jax.ShapeDtypeStruct((tokens if own else rows, features), jnp.bfloat16),
        scratch_shapes=[
            pltpu.VMEM((2, features, features), jnp.bfloat16),
            pltpu.SemaphoreType.DMA((NX,)),
        ],
        input_output_aliases=aliases,
        compiler_params=params(),
        cost_estimate=pl.CostEstimate(
            flops=4 * rows * features * features,
            bytes_accessed=6 * rows * features + 4 * features * features,
            transcendentals=0,
        ),
        name="project_own" if own else "project_other",
    )(*operands)


def carried_states(total):
    z, x, c, _ = position()
    half = total.shape[0] // 2
    peer = send(total, lambda z, x, c, y: (z, x, 1 - c, y))

    def mine(array):
        return lax.dynamic_slice_in_dim(array, c * half, half, 0)

    chip = (mine(total).astype(jnp.float32) + mine(peer).astype(jnp.float32)).astype(jnp.bfloat16)

    def along(array, place, move):
        everything = array.astype(jnp.float32)
        earlier = jnp.zeros_like(everything)
        for away in OFFSETS[1:]:
            other = send(array, functools.partial(move, away)).astype(jnp.float32)
            from_place = (place - away) % 4
            everything += other
            earlier += jnp.where(from_place < place, other, 0.0)
        return everything, earlier

    row_total, in_row = along(chip, x, lambda away, z, x, c, y: (z, x + away, c, y))
    _, in_plane = along(
        row_total.astype(jnp.bfloat16), z, lambda away, z, x, c, y: (z + away, x, c, y)
    )
    my_half = (in_row + in_plane).astype(jnp.bfloat16)
    other_half = send(my_half, lambda z, x, c, y: (z, x, 1 - c, y))
    carried = jnp.concatenate(
        [jnp.where(c == 0, my_half, other_half), jnp.where(c == 0, other_half, my_half)], axis=0
    ).astype(jnp.float32)
    return carried + jnp.where(c == 1, peer.astype(jnp.float32), 0.0)


def kept(z, y):
    return (z ^ y) in (0, 3)


def gathered_weight(weight):
    _, _, c, _ = position()
    rows = weight.shape[0] // NC

    def swap(turn, z, x, c, y):
        core = 1 - c if turn else c
        return (z, x, core, y) if kept(z, y) else (z ^ 1, x, core, y ^ 1)

    same = send(
        lax.dynamic_slice_in_dim(weight, c * rows, rows, 0), functools.partial(swap, False)
    )
    cross = send(
        lax.dynamic_slice_in_dim(weight, (1 - c) * rows, rows, 0), functools.partial(swap, True)
    )
    chip = jnp.concatenate(
        [jnp.where(c == 0, same, cross), jnp.where(c == 0, cross, same)], axis=1
    )

    def move(first, away, z, x, c, y):
        if (c == 0) == first:
            return z, x - away, c, y
        return z - away, x, c, y

    line = jnp.stack(
        [chip] + [send(chip, functools.partial(move, True, away)) for away in OFFSETS[1:]]
    )
    pieces = [line] + [send(line, functools.partial(move, False, away)) for away in OFFSETS[1:]]
    return pieces + [send(piece, lambda z, x, c, y: (z, x, 1 - c, y)) for piece in pieces]


def on_device(queries, keys, values, out_weight):
    tokens = queries.shape[0]
    pieces = gathered_weight(out_weight)
    key_feat, total, first = states(keys, values)
    carried = carried_states(total)
    start = jnp.stack([carried, carried + first]).astype(jnp.bfloat16)
    local = [local_part(queries, key_feat, values, i) for i in range(tokens // QROWS)]

    normed = [norm_part(*local[row // QROWS], start, row, rows) for row, rows in CHUNKS]
    peers = [send(chunk, lambda z, x, c, y: (z, x, c, y ^ 1)) for chunk in normed]
    partial = [project(mine, peer, pieces) for mine, peer in zip(normed, peers)]
    received = [send(chunk, lambda z, x, c, y: (z, x, c, 3 - y)) for chunk in partial]
    out = None
    for (row, _), mine, peer, other in zip(CHUNKS, normed, peers, received):
        out = project(mine, peer, pieces, other, row, tokens, out)
    return out


def solution(mesh):
    in_specs = (P("seq", "head"), P("seq", "head"), P("seq", "head"), P("head", "seq"))
    out_specs = P("seq", "head")
    return jax.shard_map(
        on_device, mesh=mesh, in_specs=in_specs, out_specs=out_specs, check_vma=False
    )
```

```python
import functools

import jax
import jax.numpy as jnp
from jax import lax
from jax.experimental import pallas as pl
from jax.experimental.pallas import tpu as pltpu
from jax.sharding import PartitionSpec as P

HEAD_DIM = 128
BLOCK = 512
EPSILON = 1e-06
AXES = ("seq", "head")
NZ, NX, NC, NY = 4, 4, 2, 4
OFFSETS = (0, 1, -1, 2)
QROWS = 256
CHUNKS = ((0, 128), (128, 128), (256, 256), (512, 256), (768, 128), (896, 128))
VMEM_LIMIT = 10 * 1024 * 1024
COST = pl.CostEstimate(flops=1, bytes_accessed=1, transcendentals=0)


def route(target):
    pairs = []
    for z in range(NZ):
        for x in range(NX):
            for c in range(NC):
                for y in range(NY):
                    z2, x2, c2, y2 = target(z, x, c, y)
                    source = ((z * NX + x) * NC + c) * NY + y
                    to = (((z2 % NZ) * NX + x2 % NX) * NC + c2) * NY + y2
                    pairs.append((source, to))
    return pairs


def send(array, target):
    return lax.ppermute(array, AXES, route(target))


def params():
    return pltpu.CompilerParams(vmem_limit_bytes=VMEM_LIMIT)


def feature(source):
    wide = source.astype(jnp.float32)
    return jnp.where(wide > 0, wide + 1.0, jnp.exp(jnp.minimum(wide, 0.0))).astype(jnp.bfloat16)


def state_kernel(keys_hbm, values_hbm, feat_ref, total_ref, first_ref, keys, values, arrived):
    groups, _, width = keys.shape
    copies = []
    for group in range(groups):
        columns = slice(group * width, (group + 1) * width)
        for index, (source, target) in enumerate(((keys_hbm, keys), (values_hbm, values))):
            copies.append(
                pltpu.make_async_copy(
                    source.at[:, columns], target.at[group], arrived.at[group, index]
                )
            )
            copies[-1].start()
    for group in range(groups):
        copies[2 * group].wait()
        copies[2 * group + 1].wait()
        for inner in range(width // HEAD_DIM):
            head = group * (width // HEAD_DIM) + inner
            here = slice(inner * HEAD_DIM, (inner + 1) * HEAD_DIM)
            feat = feature(keys[group, :, here])
            feat_ref[:, head * HEAD_DIM : (head + 1) * HEAD_DIM] = feat
            sums = []
            for block in range(2):
                rows = slice(block * BLOCK, (block + 1) * BLOCK)
                sums.append(
                    lax.dot_general(
                        feat[rows],
                        values[group, rows, here],
                        (((0,), (0,)), ((), ())),
                        preferred_element_type=jnp.float32,
                    )
                )
            first_ref[head] = sums[0]
            total_ref[head] = (sums[0] + sums[1]).astype(jnp.bfloat16)


def states(keys, values):
    tokens, features = keys.shape
    heads = features // HEAD_DIM
    groups = 4
    buffer = pltpu.VMEM((groups, tokens, features // groups), jnp.bfloat16)
    return pl.pallas_call(
        state_kernel,
        in_specs=[pl.BlockSpec(memory_space=pltpu.HBM)] * 2,
        out_shape=[
            jax.ShapeDtypeStruct((tokens, features), jnp.bfloat16),
            jax.ShapeDtypeStruct((heads, HEAD_DIM, HEAD_DIM), jnp.bfloat16),
            jax.ShapeDtypeStruct((heads, HEAD_DIM, HEAD_DIM), jnp.float32),
        ],
        scratch_shapes=[buffer, buffer, pltpu.SemaphoreType.DMA((groups, 2))],
        compiler_params=params(),
        cost_estimate=COST,
        name="states",
    )(keys, values)


def local_kernel(queries_ref, feat_ref, values_ref, local_ref, query_feat_ref):
    rows = queries_ref.shape[0]
    span = feat_ref.shape[0]
    row = lax.broadcasted_iota(jnp.int32, (rows, rows), 0)
    column = lax.broadcasted_iota(jnp.int32, (rows, rows), 1)
    causal = column <= row
    for head in range(queries_ref.shape[1] // HEAD_DIM):
        columns = slice(head * HEAD_DIM, (head + 1) * HEAD_DIM)
        query_feat = feature(queries_ref[:, columns])
        query_feat_ref[:, columns] = query_feat
        scores = lax.dot_general(
            query_feat,
            feat_ref[:, columns],
            (((1,), (1,)), ((), ())),
            preferred_element_type=jnp.float32,
        )
        diagonal = jnp.where(causal, scores[:, span - rows :], 0.0).astype(jnp.bfloat16)
        out = jnp.dot(
            diagonal, values_ref[span - rows :, columns], preferred_element_type=jnp.float32
        )
        if span > rows:
            out += jnp.dot(
                scores[:, : span - rows].astype(jnp.bfloat16),
                values_ref[: span - rows, columns],
                preferred_element_type=jnp.float32,
            )
        local_ref[:, columns] = out


def local_part(queries, key_feat, values, index):
    features = queries.shape[1]
    width = features // 2
    span = QROWS * (index % 2 + 1)
    first = (index // 2) * (BLOCK // span)
    rows = pl.BlockSpec((QROWS, width), lambda i: (index, i))
    source = pl.BlockSpec((span, width), lambda i: (first, i))
    out = pl.BlockSpec((QROWS, width), lambda i: (0, i))
    return pl.pallas_call(
        local_kernel,
        grid=(features // width,),
        in_specs=[rows, source, source],
        out_specs=[out, out],
        out_shape=[
            jax.ShapeDtypeStruct((QROWS, features), jnp.float32),
            jax.ShapeDtypeStruct((QROWS, features), jnp.bfloat16),
        ],
        compiler_params=params(),
        cost_estimate=COST,
        name="local_part",
    )(queries, key_feat, values)


def norm_kernel(local_ref, query_feat_ref, start_ref, normed_ref):
    for head in range(local_ref.shape[1] // HEAD_DIM):
        columns = slice(head * HEAD_DIM, (head + 1) * HEAD_DIM)
        combined = local_ref[:, columns] + jnp.dot(
            query_feat_ref[:, columns], start_ref[0, head], preferred_element_type=jnp.float32
        )
        mean = jnp.mean(combined * combined, axis=-1, keepdims=True)
        normed_ref[:, columns] = (combined * lax.rsqrt(mean + EPSILON)).astype(jnp.bfloat16)


def norm_part(local, query_feat, start, row, rows):
    features = local.shape[1]
    heads = features // HEAD_DIM
    block = row // BLOCK
    place = (row % QROWS) // rows
    spec = pl.BlockSpec((rows, features), lambda i: (place, 0))
    return pl.pallas_call(
        norm_kernel,
        grid=(1,),
        in_specs=[
            spec,
            spec,
            pl.BlockSpec((1, heads, HEAD_DIM, HEAD_DIM), lambda i: (block, 0, 0, 0)),
        ],
        out_specs=pl.BlockSpec((rows, features), lambda i: (0, 0)),
        out_shape=jax.ShapeDtypeStruct((rows, features), jnp.bfloat16),
        compiler_params=params(),
        cost_estimate=COST,
        name="norm_part",
    )(local, query_feat, start)


def position():
    seq = lax.axis_index("seq")
    return seq // (NX * NC), (seq // NC) % NX, seq % NC, lax.axis_index("head")


def after(value, *done):
    return lax.optimization_barrier((value, *done))[0]


def small(body, shapes, *operands, name):
    return pl.pallas_call(
        body,
        out_shape=shapes,
        compiler_params=params(),
        cost_estimate=COST,
        name=name,
    )(*operands)


def assemble_kernel(home, blocks, *refs):
    out_ref, arrived = refs[-2:]
    z, x, c, y = position()
    piece_rows, piece_columns = refs[0].shape[-2:]
    copies = []
    for number, (index, inner, place) in enumerate(blocks):
        from_z, from_x, core = place(z, x, c)
        kind = jnp.bitwise_xor(from_z, y)
        slot = jnp.where((kind == 0) | (kind == 3), 0, 1)
        second = jnp.where((kind < 2) == (home == 0), 0, 1)
        column = (from_x * NC + core) * piece_columns
        copies.append(
            pltpu.make_async_copy(
                refs[index].at[inner],
                out_ref.at[
                    slot,
                    pl.ds(pl.multiple_of(second * piece_rows, piece_rows), piece_rows),
                    pl.ds(pl.multiple_of(column, piece_columns), piece_columns),
                ],
                arrived.at[number],
            )
        )
    for copy in copies:
        copy.start()
    for copy in copies:
        copy.wait()


def assemble(home, blocks, *pieces):
    side = 2 * pieces[0].shape[-2]
    return pl.pallas_call(
        functools.partial(assemble_kernel, home, blocks),
        in_specs=[pl.BlockSpec(memory_space=pl.ANY)] * len(pieces),
        out_specs=pl.BlockSpec(memory_space=pl.ANY),
        out_shape=jax.ShapeDtypeStruct((2, side, side), jnp.bfloat16),
        scratch_shapes=[pltpu.SemaphoreType.DMA((len(blocks),))],
        compiler_params=params(),
        cost_estimate=COST,
        name="assemble",
    )(*pieces)


def project_kernel(normed_ref, peer_ref, weight_ref, out_ref, *, received_ref=None):
    total = jnp.dot(normed_ref[...], weight_ref[0], preferred_element_type=jnp.float32)
    total += jnp.dot(peer_ref[...], weight_ref[1], preferred_element_type=jnp.float32)
    if received_ref is not None:
        total += received_ref[...].astype(jnp.float32)
    out_ref[...] = total.astype(jnp.bfloat16)


def project(normed, peer, weight, received=None, row=0, tokens=0, target=None):
    rows, features = normed.shape
    own = received is not None
    chunk = pl.BlockSpec((rows, features), lambda i: (0, 0))
    place = row // rows if own else 0
    operands = [normed, peer, weight]
    specs = [chunk, chunk, pl.BlockSpec(weight.shape, lambda i: (0, 0, 0))]
    aliases = {}
    if own:
        operands.append(received)
        specs.append(chunk)
    if target is not None:
        aliases = {len(operands): 0}
        operands.append(target)
        specs.append(pl.BlockSpec(memory_space=pl.ANY))

    def body(*refs):
        project_kernel(*refs[:3], refs[-1], received_ref=refs[3] if own else None)

    return pl.pallas_call(
        body,
        grid=(1,),
        in_specs=specs,
        out_specs=pl.BlockSpec((rows, features), lambda i: (place, 0)),
        out_shape=jax.ShapeDtypeStruct((tokens if own else rows, features), jnp.bfloat16),
        input_output_aliases=aliases,
        compiler_params=params(),
        cost_estimate=COST,
        name="project_own" if own else "project_other",
    )(*operands)


def other_core(z, x, c, y):
    return z, x, 1 - c, y


def along_x(away, z, x, c, y):
    return z, x - away, c, y


def along_z(away, z, x, c, y):
    return z - away, x, c, y


def chip_kernel(total_ref, peer_ref, wide_ref, chip_ref):
    half = chip_ref.shape[0]
    mine = pl.ds(position()[2] * half, half)
    wide = total_ref[mine].astype(jnp.float32) + peer_ref[mine].astype(jnp.float32)
    wide_ref[...] = wide
    chip_ref[...] = wide.astype(jnp.bfloat16)


def step_kernel(axis, bit, *refs):
    wide_ref, other_ref, next_wide_ref, next_ref, earlier_out_ref = refs[0], *refs[-4:]
    place = position()[axis]
    other = other_ref[...].astype(jnp.float32)
    wide = wide_ref[...] + other
    earlier = jnp.where(jnp.bitwise_and(place, bit) != 0, other, 0.0)
    if len(refs) == 6:
        earlier += refs[1][...]
    next_wide_ref[...] = wide
    next_ref[...] = wide.astype(jnp.bfloat16)
    earlier_out_ref[...] = earlier


def last_kernel(earlier_ref, other_ref, half_ref):
    place = position()[0]
    other = other_ref[...].astype(jnp.float32)
    half_ref[...] = (earlier_ref[...] + jnp.where(place >= 2, other, 0.0)).astype(jnp.bfloat16)


def start_kernel(mine_ref, other_ref, peer_ref, first_ref, start_ref):
    core = position()[2]
    half = mine_ref.shape[0]
    for place in range(2):
        heads = slice(place * half, (place + 1) * half)
        carried = jnp.where(
            core == place, mine_ref[...].astype(jnp.float32), other_ref[...].astype(jnp.float32)
        )
        carried += jnp.where(core == 1, peer_ref[heads].astype(jnp.float32), 0.0)
        start_ref[0, heads] = carried.astype(jnp.bfloat16)
        start_ref[1, heads] = (carried + first_ref[heads]).astype(jnp.bfloat16)


def home(z, y):
    return (z, y) if (z ^ y) in (0, 3) else (z ^ 1, y ^ 1)


def item_kernel(a_ref, b_ref, own_ref, other_ref):
    z, _, _, y = position()
    far = jnp.bitwise_xor(z, y) >= 2
    own_ref[...] = jnp.where(far, b_ref[...], a_ref[...])
    other_ref[...] = jnp.where(far, a_ref[...], b_ref[...])


def spread_weight(weight):
    rows = weight.shape[0] // 2

    def to(second, z, x, c, y):
        z, y = home(z, y)
        return (z ^ 3 if second else z), x, c, y

    parts = [weight[:rows], weight[rows:]]
    return parts[0], [send(part, functools.partial(to, i)) for i, part in enumerate(parts)]


def first_moves(item):
    return [item] + [send(item, functools.partial(line_move, True, away)) for away in OFFSETS[1:]]


def second_moves(line):
    return [line] + [send(line, functools.partial(line_move, False, away)) for away in OFFSETS[1:]]


def line_move(first, away, z, x, c, y):
    return along_x(away, z, x, c, y) if (c == 0) == first else along_z(away, z, x, c, y)


def line_place(mine, outer, inner, z, x, c):
    core = c if mine else 1 - c
    from_z = lax.rem(z + jnp.where(core == 0, outer, inner) + NZ, NZ)
    from_x = lax.rem(x + jnp.where(core == 0, inner, outer) + NX, NX)
    return from_z, from_x, core


def pair_place(mine, outer, inner, z, x, c):
    from_z, from_x, core = line_place(True, outer, inner, z, x, c)
    return from_z, from_x, core if mine else 1 - core


PAIR_BLOCKS = [
    (index, (inner, side), functools.partial(pair_place, side == 0, OFFSETS[index], OFFSETS[inner]))
    for index in range(4)
    for inner in range(4)
    for side in range(2)
]

LINE_BLOCKS = [
    (index, inner, functools.partial(line_place, index < 4, OFFSETS[index % 4], OFFSETS[inner]))
    for index in range(8)
    for inner in range(4)
]


def on_device(queries, keys, values, out_weight):
    tokens = queries.shape[0]

    ready, parts = spread_weight(out_weight)
    key_feat, total, first = states(after(keys, ready), values)
    heads = total.shape[0]
    half = jax.ShapeDtypeStruct((heads // 2, HEAD_DIM, HEAD_DIM), jnp.bfloat16)
    wide_half = jax.ShapeDtypeStruct(half.shape, jnp.float32)

    total = after(total, *parts)
    peer = send(total, other_core)
    item = jax.ShapeDtypeStruct(parts[0].shape, parts[0].dtype)
    own_item, other_item = small(
        item_kernel, [item, item], *after(tuple(parts), total), name="weight_items"
    )

    wide, chip = small(chip_kernel, [wide_half, half], total, peer, name="chip_sum")
    other_chip = send(chip, lambda z, x, c, y: (z, x ^ 1, c, y))
    line = first_moves(after(other_item, chip))
    local = [local_part(after(queries, chip), key_feat, values, 0)]
    wide, chip, earlier = small(
        functools.partial(step_kernel, 1, 1),
        [wide_half, half, wide_half],
        wide,
        after(other_chip, local[0][0]),
        name="step_x",
    )
    other_chip = send(chip, lambda z, x, c, y: (z, 3 - x, c, y))
    wide, chip, earlier = small(
        functools.partial(step_kernel, 1, 2),
        [wide_half, half, wide_half],
        wide,
        earlier,
        other_chip,
        name="step_x2",
    )
    own_pair = jnp.stack([own_item, send(after(own_item, chip), other_core)])
    other_chip = send(chip, lambda z, x, c, y: (z ^ 1, x, c, y))
    other_chip = after(other_chip, own_pair)
    wide, chip, earlier = small(
        functools.partial(step_kernel, 0, 1),
        [wide_half, half, wide_half],
        wide,
        earlier,
        other_chip,
        name="step_z",
    )
    other_chip = send(chip, lambda z, x, c, y: (3 - z, x, c, y))
    line = jnp.stack(after(tuple(line), chip))
    lines = second_moves(line)
    my_half = small(last_kernel, half, earlier, after(other_chip, line), name="step_z2")
    other_half = send(my_half, other_core)
    start = small(
        start_kernel,
        jax.ShapeDtypeStruct((2, heads, HEAD_DIM, HEAD_DIM), jnp.bfloat16),
        my_half,
        other_half,
        peer,
        first,
        name="start_states",
    )

    normed, peers, partial = [], [], []

    def norm(index, *done):
        place, rows = CHUNKS[index]
        number = place // QROWS
        if number == len(local):
            local.append(local_part(after(queries, *done), key_feat, values, number))
        query_feat = after(local[number][1], *done) if done else local[number][1]
        normed.append(norm_part(local[number][0], query_feat, start, place, rows))
        peers.append(send(normed[-1], lambda z, x, c, y: (z, x, c, y ^ 1)))

    def other(index):
        partial.append(project(normed[index], peers[index], weight))
        return partial[-1]

    received = []

    def reply(index):
        received.append(send(partial[index], lambda z, x, c, y: (z, x, c, 3 - y)))

    received = []

    def reply(index):
        received.append(send(partial[index], lambda z, x, c, y: (z, x, c, 3 - y)))

    norm(0)
    norm(1, normed[0])
    norm(2, normed[1])
    own_line = first_moves(after(own_pair, normed[0]))
    lines = list(after(tuple(lines), peers[0], normed[2]))
    lines += [send(piece, other_core) for piece in lines]
    weight = assemble(1, LINE_BLOCKS, *lines)
    other(0)
    reply(0)
    peers[1] = after(peers[1], partial[0])
    other(1)
    reply(1)
    own_lines = second_moves(jnp.stack(after(tuple(own_line), partial[1])))
    norm(3, partial[1])
    peers[2] = after(peers[2], received[0], received[1], normed[3])
    other(2)
    reply(2)
    norm(4, partial[2])
    norm(5, normed[4])
    peers[3] = after(peers[3], normed[5])
    other(3)
    reply(3)
    peers[4] = after(peers[4], received[2], partial[3])
    other(4)
    reply(4)
    own_weight = assemble(0, PAIR_BLOCKS, *after(tuple(own_lines), partial[4]))
    out = None

    def own(index, *done):
        row = CHUNKS[index][0]
        back = after(received[index], *done) if done else received[index]
        return project(normed[index], peers[index], own_weight, back, row, tokens, out)

    for index in range(3):
        out = own(index)
    peers[5] = after(peers[5], received[3], out)
    other(5)
    reply(5)
    out = own(3, partial[5])
    out = own(4)
    return own(5)


def solution(mesh):
    in_specs = (P("seq", "head"), P("seq", "head"), P("seq", "head"), P("head", "seq"))
    out_specs = P("seq", "head")
    return jax.shard_map(
        on_device, mesh=mesh, in_specs=in_specs, out_specs=out_specs, check_vma=False
    )
```

```python
import functools

import jax
import jax.numpy as jnp
from jax import lax
from jax.experimental import pallas as pl
from jax.experimental.pallas import tpu as pltpu
from jax.sharding import PartitionSpec as P

HEAD_DIM = 128
BLOCK = 512
EPSILON = 1e-06
AXES = ("seq", "head")
NZ, NX, NC, NY = 4, 4, 2, 4
OFFSETS = (0, 1, -1, 2)
QROWS = 256
CHUNKS = ((0, 128), (128, 128), (256, 256), (512, 256), (768, 256))
VMEM_LIMIT = 10 * 1024 * 1024
COST = pl.CostEstimate(flops=1, bytes_accessed=1, transcendentals=0)


def route(target):
    pairs = []
    for z in range(NZ):
        for x in range(NX):
            for c in range(NC):
                for y in range(NY):
                    z2, x2, c2, y2 = target(z, x, c, y)
                    source = ((z * NX + x) * NC + c) * NY + y
                    to = (((z2 % NZ) * NX + x2 % NX) * NC + c2) * NY + y2
                    pairs.append((source, to))
    return pairs


def send(array, target):
    return lax.ppermute(array, AXES, route(target))


def params():
    return pltpu.CompilerParams(vmem_limit_bytes=VMEM_LIMIT)


def feature(source):
    wide = source.astype(jnp.float32)
    return jnp.where(wide > 0, wide + 1.0, jnp.exp(jnp.minimum(wide, 0.0))).astype(jnp.bfloat16)


def state_kernel(keys_hbm, values_hbm, feat_ref, total_ref, first_ref, keys, values, arrived):
    groups, _, width = keys.shape
    copies = []
    for group in range(groups):
        columns = slice(group * width, (group + 1) * width)
        for index, (source, target) in enumerate(((keys_hbm, keys), (values_hbm, values))):
            copies.append(
                pltpu.make_async_copy(
                    source.at[:, columns], target.at[group], arrived.at[group, index]
                )
            )
            copies[-1].start()
    for group in range(groups):
        copies[2 * group].wait()
        copies[2 * group + 1].wait()
        for inner in range(width // HEAD_DIM):
            head = group * (width // HEAD_DIM) + inner
            here = slice(inner * HEAD_DIM, (inner + 1) * HEAD_DIM)
            feat = feature(keys[group, :, here])
            feat_ref[:, head * HEAD_DIM : (head + 1) * HEAD_DIM] = feat
            sums = []
            for block in range(2):
                rows = slice(block * BLOCK, (block + 1) * BLOCK)
                sums.append(
                    lax.dot_general(
                        feat[rows],
                        values[group, rows, here],
                        (((0,), (0,)), ((), ())),
                        preferred_element_type=jnp.float32,
                    )
                )
            first_ref[head] = sums[0]
            total_ref[head] = (sums[0] + sums[1]).astype(jnp.bfloat16)


def states(keys, values):
    tokens, features = keys.shape
    heads = features // HEAD_DIM
    groups = 4
    buffer = pltpu.VMEM((groups, tokens, features // groups), jnp.bfloat16)
    return pl.pallas_call(
        state_kernel,
        in_specs=[pl.BlockSpec(memory_space=pltpu.HBM)] * 2,
        out_shape=[
            jax.ShapeDtypeStruct((tokens, features), jnp.bfloat16),
            jax.ShapeDtypeStruct((heads, HEAD_DIM, HEAD_DIM), jnp.bfloat16),
            jax.ShapeDtypeStruct((heads, HEAD_DIM, HEAD_DIM), jnp.float32),
        ],
        scratch_shapes=[buffer, buffer, pltpu.SemaphoreType.DMA((groups, 2))],
        compiler_params=params(),
        cost_estimate=COST,
        name="states",
    )(keys, values)


def local_kernel(queries_ref, feat_ref, values_ref, local_ref, query_feat_ref):
    rows = queries_ref.shape[0]
    span = feat_ref.shape[0]
    row = lax.broadcasted_iota(jnp.int32, (rows, rows), 0)
    column = lax.broadcasted_iota(jnp.int32, (rows, rows), 1)
    causal = column <= row
    for head in range(queries_ref.shape[1] // HEAD_DIM):
        columns = slice(head * HEAD_DIM, (head + 1) * HEAD_DIM)
        query_feat = feature(queries_ref[:, columns])
        query_feat_ref[:, columns] = query_feat
        scores = lax.dot_general(
            query_feat,
            feat_ref[:, columns],
            (((1,), (1,)), ((), ())),
            preferred_element_type=jnp.float32,
        )
        diagonal = jnp.where(causal, scores[:, span - rows :], 0.0).astype(jnp.bfloat16)
        out = jnp.dot(
            diagonal, values_ref[span - rows :, columns], preferred_element_type=jnp.float32
        )
        if span > rows:
            out += jnp.dot(
                scores[:, : span - rows].astype(jnp.bfloat16),
                values_ref[: span - rows, columns],
                preferred_element_type=jnp.float32,
            )
        local_ref[:, columns] = out


def local_part(queries, key_feat, values, index):
    features = queries.shape[1]
    width = features // 2
    span = QROWS * (index % 2 + 1)
    first = (index // 2) * (BLOCK // span)
    rows = pl.BlockSpec((QROWS, width), lambda i: (index, i))
    source = pl.BlockSpec((span, width), lambda i: (first, i))
    out = pl.BlockSpec((QROWS, width), lambda i: (0, i))
    return pl.pallas_call(
        local_kernel,
        grid=(features // width,),
        in_specs=[rows, source, source],
        out_specs=[out, out],
        out_shape=[
            jax.ShapeDtypeStruct((QROWS, features), jnp.float32),
            jax.ShapeDtypeStruct((QROWS, features), jnp.bfloat16),
        ],
        compiler_params=params(),
        cost_estimate=COST,
        name="local_part",
    )(queries, key_feat, values)


def norm_kernel(local_ref, query_feat_ref, start_ref, normed_ref):
    for head in range(local_ref.shape[1] // HEAD_DIM):
        columns = slice(head * HEAD_DIM, (head + 1) * HEAD_DIM)
        combined = local_ref[:, columns] + jnp.dot(
            query_feat_ref[:, columns], start_ref[0, head], preferred_element_type=jnp.float32
        )
        mean = jnp.mean(combined * combined, axis=-1, keepdims=True)
        normed_ref[:, columns] = (combined * lax.rsqrt(mean + EPSILON)).astype(jnp.bfloat16)


def norm_part(local, query_feat, start, row, rows):
    features = local.shape[1]
    heads = features // HEAD_DIM
    block = row // BLOCK
    place = (row % QROWS) // rows
    spec = pl.BlockSpec((rows, features), lambda i: (place, 0))
    return pl.pallas_call(
        norm_kernel,
        grid=(1,),
        in_specs=[
            spec,
            spec,
            pl.BlockSpec((1, heads, HEAD_DIM, HEAD_DIM), lambda i: (block, 0, 0, 0)),
        ],
        out_specs=pl.BlockSpec((rows, features), lambda i: (0, 0)),
        out_shape=jax.ShapeDtypeStruct((rows, features), jnp.bfloat16),
        compiler_params=params(),
        cost_estimate=COST,
        name="norm_part",
    )(local, query_feat, start)


def position():
    seq = lax.axis_index("seq")
    return seq // (NX * NC), (seq // NC) % NX, seq % NC, lax.axis_index("head")


def after(value, *done):
    return lax.optimization_barrier((value, *done))[0]


def small(body, shapes, *operands, name):
    return pl.pallas_call(
        body,
        out_shape=shapes,
        compiler_params=params(),
        cost_estimate=COST,
        name=name,
    )(*operands)


def assemble_kernel(home, blocks, *refs):
    out_ref, arrived = refs[-2:]
    z, x, c, y = position()
    piece_rows, piece_columns = refs[0].shape[-2:]
    copies = []
    for number, (index, inner, place) in enumerate(blocks):
        from_z, from_x, core = place(z, x, c)
        kind = jnp.bitwise_xor(from_z, y)
        slot = jnp.where((kind == 0) | (kind == 3), 0, 1)
        second = jnp.where((kind < 2) == (home == 0), 0, 1)
        column = (from_x * NC + core) * piece_columns
        copies.append(
            pltpu.make_async_copy(
                refs[index].at[inner],
                out_ref.at[
                    slot,
                    pl.ds(pl.multiple_of(second * piece_rows, piece_rows), piece_rows),
                    pl.ds(pl.multiple_of(column, piece_columns), piece_columns),
                ],
                arrived.at[number],
            )
        )
    for copy in copies:
        copy.start()
    for copy in copies:
        copy.wait()


def assemble(home, blocks, *pieces):
    side = 2 * pieces[0].shape[-2]
    return pl.pallas_call(
        functools.partial(assemble_kernel, home, blocks),
        in_specs=[pl.BlockSpec(memory_space=pl.ANY)] * len(pieces),
        out_specs=pl.BlockSpec(memory_space=pl.ANY),
        out_shape=jax.ShapeDtypeStruct((2, side, side), jnp.bfloat16),
        scratch_shapes=[pltpu.SemaphoreType.DMA((len(blocks),))],
        compiler_params=params(),
        cost_estimate=COST,
        name="assemble",
    )(*pieces)


def project_kernel(normed_ref, peer_ref, weight_ref, out_ref, *, received_ref=None):
    total = jnp.dot(normed_ref[...], weight_ref[0], preferred_element_type=jnp.float32)
    total += jnp.dot(peer_ref[...], weight_ref[1], preferred_element_type=jnp.float32)
    if received_ref is not None:
        total += received_ref[...].astype(jnp.float32)
    out_ref[...] = total.astype(jnp.bfloat16)


def project(normed, peer, weight, received=None, row=0, tokens=0, target=None):
    rows, features = normed.shape
    own = received is not None
    chunk = pl.BlockSpec((rows, features), lambda i: (0, 0))
    place = row // rows if own else 0
    operands = [normed, peer, weight]
    specs = [chunk, chunk, pl.BlockSpec(weight.shape, lambda i: (0, 0, 0))]
    aliases = {}
    if own:
        operands.append(received)
        specs.append(chunk)
    if target is not None:
        aliases = {len(operands): 0}
        operands.append(target)
        specs.append(pl.BlockSpec(memory_space=pl.ANY))

    def body(*refs):
        project_kernel(*refs[:3], refs[-1], received_ref=refs[3] if own else None)

    return pl.pallas_call(
        body,
        grid=(1,),
        in_specs=specs,
        out_specs=pl.BlockSpec((rows, features), lambda i: (place, 0)),
        out_shape=jax.ShapeDtypeStruct((tokens if own else rows, features), jnp.bfloat16),
        input_output_aliases=aliases,
        compiler_params=params(),
        cost_estimate=COST,
        name="project_own" if own else "project_other",
    )(*operands)


def other_core(z, x, c, y):
    return z, x, 1 - c, y


def along_x(away, z, x, c, y):
    return z, x - away, c, y


def along_z(away, z, x, c, y):
    return z - away, x, c, y


def chip_kernel(total_ref, peer_ref, wide_ref, chip_ref):
    half = chip_ref.shape[0]
    mine = pl.ds(position()[2] * half, half)
    wide = total_ref[mine].astype(jnp.float32) + peer_ref[mine].astype(jnp.float32)
    wide_ref[...] = wide
    chip_ref[...] = wide.astype(jnp.bfloat16)


def step_kernel(axis, bit, *refs):
    wide_ref, other_ref, next_wide_ref, next_ref, earlier_out_ref = refs[0], *refs[-4:]
    place = position()[axis]
    other = other_ref[...].astype(jnp.float32)
    wide = wide_ref[...] + other
    earlier = jnp.where(jnp.bitwise_and(place, bit) != 0, other, 0.0)
    if len(refs) == 6:
        earlier += refs[1][...]
    next_wide_ref[...] = wide
    next_ref[...] = wide.astype(jnp.bfloat16)
    earlier_out_ref[...] = earlier


def last_kernel(earlier_ref, other_ref, half_ref):
    place = position()[0]
    other = other_ref[...].astype(jnp.float32)
    half_ref[...] = (earlier_ref[...] + jnp.where(place >= 2, other, 0.0)).astype(jnp.bfloat16)


def start_kernel(mine_ref, other_ref, peer_ref, first_ref, start_ref):
    core = position()[2]
    half = mine_ref.shape[0]
    for place in range(2):
        heads = slice(place * half, (place + 1) * half)
        carried = jnp.where(
            core == place, mine_ref[...].astype(jnp.float32), other_ref[...].astype(jnp.float32)
        )
        carried += jnp.where(core == 1, peer_ref[heads].astype(jnp.float32), 0.0)
        start_ref[0, heads] = carried.astype(jnp.bfloat16)
        start_ref[1, heads] = (carried + first_ref[heads]).astype(jnp.bfloat16)


def home(z, y):
    return (z, y) if (z ^ y) in (0, 3) else (z ^ 1, y ^ 1)


def item_kernel(a_ref, b_ref, own_ref, other_ref):
    z, _, _, y = position()
    far = jnp.bitwise_xor(z, y) >= 2
    own_ref[...] = jnp.where(far, b_ref[...], a_ref[...])
    other_ref[...] = jnp.where(far, a_ref[...], b_ref[...])


def spread_weight(weight):
    rows = weight.shape[0] // 2

    def to(second, z, x, c, y):
        z, y = home(z, y)
        return (z ^ 3 if second else z), x, c, y

    parts = [weight[:rows], weight[rows:]]
    return parts[0], [send(part, functools.partial(to, i)) for i, part in enumerate(parts)]


def first_moves(item):
    return [item] + [send(item, functools.partial(line_move, True, away)) for away in OFFSETS[1:]]


def second_moves(line):
    return [line] + [send(line, functools.partial(line_move, False, away)) for away in OFFSETS[1:]]


def line_move(first, away, z, x, c, y):
    return along_x(away, z, x, c, y) if (c == 0) == first else along_z(away, z, x, c, y)


def line_place(mine, outer, inner, z, x, c):
    core = c if mine else 1 - c
    from_z = lax.rem(z + jnp.where(core == 0, outer, inner) + NZ, NZ)
    from_x = lax.rem(x + jnp.where(core == 0, inner, outer) + NX, NX)
    return from_z, from_x, core


def pair_place(mine, outer, inner, z, x, c):
    from_z, from_x, core = line_place(True, outer, inner, z, x, c)
    return from_z, from_x, core if mine else 1 - core


PAIR_BLOCKS = [
    (index, (inner, side), functools.partial(pair_place, side == 0, OFFSETS[index], OFFSETS[inner]))
    for index in range(4)
    for inner in range(4)
    for side in range(2)
]

LINE_BLOCKS = [
    (index, inner, functools.partial(line_place, index < 4, OFFSETS[index % 4], OFFSETS[inner]))
    for index in range(8)
    for inner in range(4)
]


def on_device(queries, keys, values, out_weight):
    tokens = queries.shape[0]

    key_feat, total, first = states(keys, values)
    _, parts = spread_weight(after(out_weight, total))
    heads = total.shape[0]
    half = jax.ShapeDtypeStruct((heads // 2, HEAD_DIM, HEAD_DIM), jnp.bfloat16)
    wide_half = jax.ShapeDtypeStruct(half.shape, jnp.float32)

    peer = send(total, other_core)
    wide, chip = small(chip_kernel, [wide_half, half], total, peer, name="chip_sum")
    other_chip = send(chip, lambda z, x, c, y: (z, x ^ 1, c, y))
    local = [local_part(after(queries, chip), key_feat, values, 0)]
    wide, chip, earlier = small(
        functools.partial(step_kernel, 1, 1),
        [wide_half, half, wide_half],
        wide,
        after(other_chip, local[0][0]),
        name="step_x",
    )
    other_chip = send(chip, lambda z, x, c, y: (z, 3 - x, c, y))
    item = jax.ShapeDtypeStruct(parts[0].shape, parts[0].dtype)
    own_item, other_item = small(
        item_kernel, [item, item], *after(tuple(parts), chip), name="weight_items"
    )
    line = first_moves(other_item)
    other_chip = after(other_chip, other_item)
    wide, chip, earlier = small(
        functools.partial(step_kernel, 1, 2),
        [wide_half, half, wide_half],
        wide,
        earlier,
        other_chip,
        name="step_x2",
    )
    other_chip = send(chip, lambda z, x, c, y: (z ^ 1, x, c, y))
    wide, chip, earlier = small(
        functools.partial(step_kernel, 0, 1),
        [wide_half, half, wide_half],
        wide,
        earlier,
        other_chip,
        name="step_z",
    )
    other_chip = send(chip, lambda z, x, c, y: (3 - z, x, c, y))
    line = jnp.stack(after(tuple(line), chip))
    lines = second_moves(line)
    my_half = small(last_kernel, half, earlier, after(other_chip, line), name="step_z2")
    other_half = send(my_half, other_core)
    start = small(
        start_kernel,
        jax.ShapeDtypeStruct((2, heads, HEAD_DIM, HEAD_DIM), jnp.bfloat16),
        my_half,
        other_half,
        peer,
        first,
        name="start_states",
    )

    normed, peers, partial = [], [], []

    def norm(index, *done):
        place, rows = CHUNKS[index]
        number = place // QROWS
        if number == len(local):
            local.append(local_part(after(queries, *done), key_feat, values, number))
        query_feat = after(local[number][1], *done) if done else local[number][1]
        normed.append(norm_part(local[number][0], query_feat, start, place, rows))
        peers.append(send(normed[-1], lambda z, x, c, y: (z, x, c, y ^ 1)))

    def other(index):
        partial.append(project(normed[index], peers[index], weight))
        return partial[-1]

    received = []

    def reply(index):
        received.append(send(partial[index], lambda z, x, c, y: (z, x, c, 3 - y)))

    received = []

    def reply(index):
        received.append(send(partial[index], lambda z, x, c, y: (z, x, c, 3 - y)))

    received = []

    def reply(index):
        received.append(send(partial[index], lambda z, x, c, y: (z, x, c, 3 - y)))

    norm(0)
    norm(1, normed[0])
    norm(2, normed[1])
    norm(3, normed[2])
    norm(4, normed[3])
    lines = list(after(tuple(lines), peers[0], peers[1], normed[4]))
    swapped = [send(piece, other_core) for piece in lines]
    weight = assemble(1, LINE_BLOCKS, *lines, *swapped)
    other(0)
    reply(0)
    peers[1] = after(peers[1], partial[0])
    other(1)
    reply(1)
    own_pair = jnp.stack([own_item, send(after(own_item, partial[1]), other_core)])
    own_line = first_moves(own_pair)
    peers[2] = after(peers[2], received[0], normed[4])
    other(2)
    reply(2)
    own_lines = second_moves(jnp.stack(after(tuple(own_line), partial[2], received[1])))
    peers[3] = after(peers[3], partial[2], received[1])
    other(3)
    reply(3)
    peers[4] = after(peers[4], received[2], partial[3])
    other(4)
    reply(4)
    own_weight = assemble(0, PAIR_BLOCKS, *after(tuple(own_lines), partial[4]))
    out = None
    for (row, _), mine, peer, back in zip(CHUNKS, normed, peers, received):
        out = project(mine, peer, own_weight, back, row, tokens, out)
    return out


def solution(mesh):
    in_specs = (P("seq", "head"), P("seq", "head"), P("seq", "head"), P("head", "seq"))
    out_specs = P("seq", "head")
    return jax.shard_map(
        on_device, mesh=mesh, in_specs=in_specs, out_specs=out_specs, check_vma=False
    )
```

```python
import functools

import jax
import jax.numpy as jnp
from jax import lax
from jax.experimental import pallas as pl
from jax.experimental.pallas import tpu as pltpu
from jax.sharding import PartitionSpec as P

HEAD_DIM = 128
BLOCK = 512
EPSILON = 1e-06
AXES = ("seq", "head")
NZ, NX, NC, NY = 4, 4, 2, 4
OFFSETS = (0, 1, -1, 2)
QROWS = 256
CHUNKS = ((0, 128), (128, 128), (256, 256), (512, 256), (768, 256))
VMEM_LIMIT = 10 * 1024 * 1024
COST = pl.CostEstimate(flops=1, bytes_accessed=1, transcendentals=0)


def route(target):
    pairs = []
    for z in range(NZ):
        for x in range(NX):
            for c in range(NC):
                for y in range(NY):
                    z2, x2, c2, y2 = target(z, x, c, y)
                    source = ((z * NX + x) * NC + c) * NY + y
                    to = (((z2 % NZ) * NX + x2 % NX) * NC + c2) * NY + y2
                    pairs.append((source, to))
    return pairs


def send(array, target):
    return lax.ppermute(array, AXES, route(target))


def params():
    return pltpu.CompilerParams(vmem_limit_bytes=VMEM_LIMIT)


def feature(source):
    wide = source.astype(jnp.float32)
    return jnp.where(wide > 0, wide + 1.0, jnp.exp(jnp.minimum(wide, 0.0))).astype(jnp.bfloat16)


def state_kernel(keys_hbm, values_hbm, feat_ref, total_ref, first_ref, keys, values, arrived):
    groups, _, width = keys.shape
    copies = []
    for group in range(groups):
        columns = slice(group * width, (group + 1) * width)
        for index, (source, target) in enumerate(((keys_hbm, keys), (values_hbm, values))):
            copies.append(
                pltpu.make_async_copy(
                    source.at[:, columns], target.at[group], arrived.at[group, index]
                )
            )
            copies[-1].start()
    for group in range(groups):
        copies[2 * group].wait()
        copies[2 * group + 1].wait()
        for inner in range(width // HEAD_DIM):
            head = group * (width // HEAD_DIM) + inner
            here = slice(inner * HEAD_DIM, (inner + 1) * HEAD_DIM)
            feat = feature(keys[group, :, here])
            feat_ref[:, head * HEAD_DIM : (head + 1) * HEAD_DIM] = feat
            sums = []
            for block in range(2):
                rows = slice(block * BLOCK, (block + 1) * BLOCK)
                sums.append(
                    lax.dot_general(
                        feat[rows],
                        values[group, rows, here],
                        (((0,), (0,)), ((), ())),
                        preferred_element_type=jnp.float32,
                    )
                )
            first_ref[head] = sums[0]
            total_ref[head] = (sums[0] + sums[1]).astype(jnp.bfloat16)


def states(keys, values):
    tokens, features = keys.shape
    heads = features // HEAD_DIM
    groups = 4
    buffer = pltpu.VMEM((groups, tokens, features // groups), jnp.bfloat16)
    return pl.pallas_call(
        state_kernel,
        in_specs=[pl.BlockSpec(memory_space=pltpu.HBM)] * 2,
        out_shape=[
            jax.ShapeDtypeStruct((tokens, features), jnp.bfloat16),
            jax.ShapeDtypeStruct((heads, HEAD_DIM, HEAD_DIM), jnp.bfloat16),
            jax.ShapeDtypeStruct((heads, HEAD_DIM, HEAD_DIM), jnp.float32),
        ],
        scratch_shapes=[buffer, buffer, pltpu.SemaphoreType.DMA((groups, 2))],
        compiler_params=params(),
        cost_estimate=COST,
        name="states",
    )(keys, values)


def local_kernel(queries_ref, feat_ref, values_ref, local_ref, query_feat_ref):
    rows = queries_ref.shape[0]
    span = feat_ref.shape[0]
    row = lax.broadcasted_iota(jnp.int32, (rows, rows), 0)
    column = lax.broadcasted_iota(jnp.int32, (rows, rows), 1)
    causal = column <= row
    for head in range(queries_ref.shape[1] // HEAD_DIM):
        columns = slice(head * HEAD_DIM, (head + 1) * HEAD_DIM)
        query_feat = feature(queries_ref[:, columns])
        query_feat_ref[:, columns] = query_feat
        scores = lax.dot_general(
            query_feat,
            feat_ref[:, columns],
            (((1,), (1,)), ((), ())),
            preferred_element_type=jnp.float32,
        )
        diagonal = jnp.where(causal, scores[:, span - rows :], 0.0).astype(jnp.bfloat16)
        out = jnp.dot(
            diagonal, values_ref[span - rows :, columns], preferred_element_type=jnp.float32
        )
        if span > rows:
            out += jnp.dot(
                scores[:, : span - rows].astype(jnp.bfloat16),
                values_ref[: span - rows, columns],
                preferred_element_type=jnp.float32,
            )
        local_ref[:, columns] = out


def local_part(queries, key_feat, values, index):
    features = queries.shape[1]
    width = features // 2
    span = QROWS * (index % 2 + 1)
    first = (index // 2) * (BLOCK // span)
    rows = pl.BlockSpec((QROWS, width), lambda i: (index, i))
    source = pl.BlockSpec((span, width), lambda i: (first, i))
    out = pl.BlockSpec((QROWS, width), lambda i: (0, i))
    return pl.pallas_call(
        local_kernel,
        grid=(features // width,),
        in_specs=[rows, source, source],
        out_specs=[out, out],
        out_shape=[
            jax.ShapeDtypeStruct((QROWS, features), jnp.float32),
            jax.ShapeDtypeStruct((QROWS, features), jnp.bfloat16),
        ],
        compiler_params=params(),
        cost_estimate=COST,
        name="local_part",
    )(queries, key_feat, values)


def norm_kernel(local_ref, query_feat_ref, start_ref, normed_ref):
    for head in range(local_ref.shape[1] // HEAD_DIM):
        columns = slice(head * HEAD_DIM, (head + 1) * HEAD_DIM)
        combined = local_ref[:, columns] + jnp.dot(
            query_feat_ref[:, columns], start_ref[0, head], preferred_element_type=jnp.float32
        )
        mean = jnp.mean(combined * combined, axis=-1, keepdims=True)
        normed_ref[:, columns] = (combined * lax.rsqrt(mean + EPSILON)).astype(jnp.bfloat16)


def norm_part(local, query_feat, start, row, rows):
    features = local.shape[1]
    heads = features // HEAD_DIM
    block = row // BLOCK
    place = (row % QROWS) // rows
    spec = pl.BlockSpec((rows, features), lambda i: (place, 0))
    return pl.pallas_call(
        norm_kernel,
        grid=(1,),
        in_specs=[
            spec,
            spec,
            pl.BlockSpec((1, heads, HEAD_DIM, HEAD_DIM), lambda i: (block, 0, 0, 0)),
        ],
        out_specs=pl.BlockSpec((rows, features), lambda i: (0, 0)),
        out_shape=jax.ShapeDtypeStruct((rows, features), jnp.bfloat16),
        compiler_params=params(),
        cost_estimate=COST,
        name="norm_part",
    )(local, query_feat, start)


def position():
    seq = lax.axis_index("seq")
    return seq // (NX * NC), (seq // NC) % NX, seq % NC, lax.axis_index("head")


def after(value, *done):
    return lax.optimization_barrier((value, *done))[0]


def small(body, shapes, *operands, name):
    return pl.pallas_call(
        body,
        out_shape=shapes,
        compiler_params=params(),
        cost_estimate=COST,
        name=name,
    )(*operands)


def assemble_kernel(home, blocks, *refs):
    out_ref, arrived = refs[-2:]
    z, x, c, y = position()
    piece_rows, piece_columns = refs[0].shape[-2:]
    copies = []
    for number, (index, inner, place) in enumerate(blocks):
        from_z, from_x, core = place(z, x, c)
        kind = jnp.bitwise_xor(from_z, y)
        slot = jnp.where((kind == 0) | (kind == 3), 0, 1)
        second = jnp.where((kind < 2) == (home == 0), 0, 1)
        column = (from_x * NC + core) * piece_columns
        copies.append(
            pltpu.make_async_copy(
                refs[index].at[inner],
                out_ref.at[
                    slot,
                    pl.ds(pl.multiple_of(second * piece_rows, piece_rows), piece_rows),
                    pl.ds(pl.multiple_of(column, piece_columns), piece_columns),
                ],
                arrived.at[number],
            )
        )
    for copy in copies:
        copy.start()
    for copy in copies:
        copy.wait()


def assemble(home, blocks, *pieces):
    side = 2 * pieces[0].shape[-2]
    return pl.pallas_call(
        functools.partial(assemble_kernel, home, blocks),
        in_specs=[pl.BlockSpec(memory_space=pl.ANY)] * len(pieces),
        out_specs=pl.BlockSpec(memory_space=pl.ANY),
        out_shape=jax.ShapeDtypeStruct((2, side, side), jnp.bfloat16),
        scratch_shapes=[pltpu.SemaphoreType.DMA((len(blocks),))],
        compiler_params=params(),
        cost_estimate=COST,
        name="assemble",
    )(*pieces)


def product(normed_ref, peer_ref, weight_ref):
    total = jnp.dot(normed_ref[...], weight_ref[0], preferred_element_type=jnp.float32)
    return total + jnp.dot(peer_ref[...], weight_ref[1], preferred_element_type=jnp.float32)


def other_kernel(normed_ref, peer_ref, weight_ref, *out_refs):
    total = product(normed_ref, peer_ref, weight_ref).astype(jnp.bfloat16)
    rows = out_refs[0].shape[0]
    for index, out_ref in enumerate(out_refs):
        out_ref[...] = total[index * rows : (index + 1) * rows]


def project_other(normed, peer, weight, parts):
    rows, features = normed.shape
    out = jax.ShapeDtypeStruct((rows // parts, features), jnp.bfloat16)
    return pl.pallas_call(
        other_kernel,
        out_shape=[out] * parts,
        compiler_params=params(),
        cost_estimate=COST,
        name="project_other",
    )(normed, peer, weight)


def own_kernel(parts, normed_refs, peer_refs, weight_ref, received_refs, out_ref):
    row = 0
    received_refs = list(received_refs)
    for count, normed_ref, peer_ref in zip(parts, normed_refs, peer_refs):
        total = product(normed_ref, peer_ref, weight_ref)
        place = 0
        for _ in range(count):
            back_ref = received_refs.pop(0)
            rows = back_ref.shape[0]
            done = total[place : place + rows] + back_ref[...].astype(jnp.float32)
            out_ref[row : row + rows] = done.astype(jnp.bfloat16)
            place += rows
            row += rows


def project_own(normed, peers, weight, received, place, tokens, target):
    features = weight.shape[-1]
    rows = sum(chunk.shape[0] for chunk in normed)
    parts = [len(group) for group in received]
    flat = [part for group in received for part in group]
    count = len(normed)
    operands = [*normed, *peers, weight, *flat]
    specs = [pl.BlockSpec(array.shape, lambda i, n=array.ndim: (0,) * n) for array in operands]
    aliases = {}
    if target is not None:
        aliases = {len(operands): 0}
        operands.append(target)
        specs.append(pl.BlockSpec(memory_space=pl.ANY))

    def body(*refs):
        back = refs[2 * count + 1 : 2 * count + 1 + len(flat)]
        own_kernel(parts, refs[:count], refs[count : 2 * count], refs[2 * count], back, refs[-1])

    return pl.pallas_call(
        body,
        grid=(1,),
        in_specs=specs,
        out_specs=pl.BlockSpec((rows, features), lambda i: (place // rows, 0)),
        out_shape=jax.ShapeDtypeStruct((tokens, features), jnp.bfloat16),
        input_output_aliases=aliases,
        compiler_params=params(),
        cost_estimate=COST,
        name="project_own",
    )(*operands)


def other_core(z, x, c, y):
    return z, x, 1 - c, y


def along_x(away, z, x, c, y):
    return z, x - away, c, y


def along_z(away, z, x, c, y):
    return z - away, x, c, y


def chip_kernel(total_ref, peer_ref, wide_ref, chip_ref):
    half = chip_ref.shape[0]
    mine = pl.ds(position()[2] * half, half)
    wide = total_ref[mine].astype(jnp.float32) + peer_ref[mine].astype(jnp.float32)
    wide_ref[...] = wide
    chip_ref[...] = wide.astype(jnp.bfloat16)


def step_kernel(axis, bit, *refs):
    wide_ref, other_ref, next_wide_ref, next_ref, earlier_out_ref = refs[0], *refs[-4:]
    place = position()[axis]
    other = other_ref[...].astype(jnp.float32)
    wide = wide_ref[...] + other
    earlier = jnp.where(jnp.bitwise_and(place, bit) != 0, other, 0.0)
    if len(refs) == 6:
        earlier += refs[1][...]
    next_wide_ref[...] = wide
    next_ref[...] = wide.astype(jnp.bfloat16)
    earlier_out_ref[...] = earlier


def last_kernel(earlier_ref, other_ref, half_ref):
    place = position()[0]
    other = other_ref[...].astype(jnp.float32)
    half_ref[...] = (earlier_ref[...] + jnp.where(place >= 2, other, 0.0)).astype(jnp.bfloat16)


def start_kernel(mine_ref, other_ref, peer_ref, first_ref, start_ref):
    core = position()[2]
    half = mine_ref.shape[0]
    for place in range(2):
        heads = slice(place * half, (place + 1) * half)
        carried = jnp.where(
            core == place, mine_ref[...].astype(jnp.float32), other_ref[...].astype(jnp.float32)
        )
        carried += jnp.where(core == 1, peer_ref[heads].astype(jnp.float32), 0.0)
        start_ref[0, heads] = carried.astype(jnp.bfloat16)
        start_ref[1, heads] = (carried + first_ref[heads]).astype(jnp.bfloat16)


def home(z, y):
    return (z, y) if (z ^ y) in (0, 3) else (z ^ 1, y ^ 1)


def item_kernel(a_ref, b_ref, own_ref, other_ref):
    z, _, _, y = position()
    far = jnp.bitwise_xor(z, y) >= 2
    own_ref[...] = jnp.where(far, b_ref[...], a_ref[...])
    other_ref[...] = jnp.where(far, a_ref[...], b_ref[...])


def spread_weight(weight):
    rows = weight.shape[0] // 2

    def to(second, z, x, c, y):
        z, y = home(z, y)
        return (z ^ 3 if second else z), x, c, y

    parts = [weight[:rows], weight[rows:]]
    return parts[0], [send(part, functools.partial(to, i)) for i, part in enumerate(parts)]


def first_moves(item):
    return [item] + [send(item, functools.partial(line_move, True, away)) for away in OFFSETS[1:]]


def paced_moves(item, first):
    near = [send(item, functools.partial(line_move, first, away)) for away in OFFSETS[1:3]]
    far = send(after(item, *near), functools.partial(line_move, first, OFFSETS[3]))
    return [item, *near, far]


def second_moves(line):
    return [line] + [send(line, functools.partial(line_move, False, away)) for away in OFFSETS[1:]]


def line_move(first, away, z, x, c, y):
    return along_x(away, z, x, c, y) if (c == 0) == first else along_z(away, z, x, c, y)


def line_place(mine, outer, inner, z, x, c):
    core = c if mine else 1 - c
    from_z = lax.rem(z + jnp.where(core == 0, outer, inner) + NZ, NZ)
    from_x = lax.rem(x + jnp.where(core == 0, inner, outer) + NX, NX)
    return from_z, from_x, core


def pair_place(mine, outer, inner, z, x, c):
    from_z, from_x, core = line_place(True, outer, inner, z, x, c)
    return from_z, from_x, core if mine else 1 - core


PAIR_BLOCKS = [
    (index, (inner, side), functools.partial(pair_place, side == 0, OFFSETS[index], OFFSETS[inner]))
    for index in range(4)
    for inner in range(4)
    for side in range(2)
]

LINE_BLOCKS = [
    (index, inner, functools.partial(line_place, index < 4, OFFSETS[index % 4], OFFSETS[inner]))
    for index in range(8)
    for inner in range(4)
]


def on_device(queries, keys, values, out_weight):
    tokens = queries.shape[0]

    key_feat, total, first = states(keys, values)
    _, parts = spread_weight(after(out_weight, total))
    heads = total.shape[0]
    half = jax.ShapeDtypeStruct((heads // 2, HEAD_DIM, HEAD_DIM), jnp.bfloat16)
    wide_half = jax.ShapeDtypeStruct(half.shape, jnp.float32)

    peer = send(total, other_core)
    wide, chip = small(chip_kernel, [wide_half, half], total, peer, name="chip_sum")
    other_chip = send(chip, lambda z, x, c, y: (z, x ^ 1, c, y))
    local = [local_part(after(queries, chip), key_feat, values, 0)]
    wide, chip, earlier = small(
        functools.partial(step_kernel, 1, 1),
        [wide_half, half, wide_half],
        wide,
        after(other_chip, local[0][0]),
        name="step_x",
    )
    other_chip = send(chip, lambda z, x, c, y: (z, 3 - x, c, y))
    item = jax.ShapeDtypeStruct(parts[0].shape, parts[0].dtype)
    own_item, other_item = small(
        item_kernel, [item, item], *after(tuple(parts), chip), name="weight_items"
    )
    line = first_moves(other_item)
    other_chip = after(other_chip, other_item)
    wide, chip, earlier = small(
        functools.partial(step_kernel, 1, 2),
        [wide_half, half, wide_half],
        wide,
        earlier,
        other_chip,
        name="step_x2",
    )
    other_chip = send(chip, lambda z, x, c, y: (z ^ 1, x, c, y))
    wide, chip, earlier = small(
        functools.partial(step_kernel, 0, 1),
        [wide_half, half, wide_half],
        wide,
        earlier,
        other_chip,
        name="step_z",
    )
    other_chip = send(chip, lambda z, x, c, y: (3 - z, x, c, y))
    line = jnp.stack(after(tuple(line), chip))
    lines = second_moves(line)
    my_half = small(last_kernel, half, earlier, after(other_chip, line), name="step_z2")
    other_half = send(my_half, other_core)
    start = small(
        start_kernel,
        jax.ShapeDtypeStruct((2, heads, HEAD_DIM, HEAD_DIM), jnp.bfloat16),
        my_half,
        other_half,
        peer,
        first,
        name="start_states",
    )

    normed, peers, partial, received = [], [], [], []
    parts = (1, 1, 1, 1, 1)

    def norm(index, *done):
        place, rows = CHUNKS[index]
        number = place // QROWS
        if number == len(local):
            local.append(local_part(after(queries, *done), key_feat, values, number))
        query_feat = after(local[number][1], *done) if done else local[number][1]
        normed.append(norm_part(local[number][0], query_feat, start, place, rows))
        ready = after(normed[-1], peers[1]) if index == 2 else normed[-1]
        peers.append(send(ready, lambda z, x, c, y: (z, x, c, y ^ 1)))

    def other(index, *done):
        if done:
            peers[index] = after(peers[index], *done)
        partial.append(project_other(normed[index], peers[index], weight, parts[index]))
        received.append(
            [send(part, lambda z, x, c, y: (z, x, c, 3 - y)) for part in partial[index]]
        )

    norm(0)
    norm(1, normed[0])
    norm(2, normed[1])
    norm(3, normed[2])
    lines = list(after(tuple(lines), peers[0], normed[3]))
    swapped = [send(piece, other_core) for piece in lines]
    weight = assemble(1, LINE_BLOCKS, *lines, *swapped)
    other(0)
    norm(4, partial[0][0])
    other(1, normed[4])
    own_pair = jnp.stack([own_item, send(after(own_item, partial[1][0]), other_core)])
    own_line = first_moves(own_pair)
    other(2, received[0][0], normed[4])
    own_lines = second_moves(jnp.stack(after(tuple(own_line), partial[2][0], received[1][0])))
    other(3, partial[2][0], received[1][0], received[2][0])
    other(4, partial[3][0])
    own_weight = assemble(0, PAIR_BLOCKS, *after(tuple(own_lines), partial[4][0]))
    out = project_own(normed[:4], peers[:4], own_weight, received[:4], 0, tokens, None)
    return project_own(
        normed[4:], peers[4:], own_weight, received[4:], CHUNKS[4][0], tokens, out
    )


def solution(mesh):
    in_specs = (P("seq", "head"), P("seq", "head"), P("seq", "head"), P("head", "seq"))
    out_specs = P("seq", "head")
    return jax.shard_map(
        on_device, mesh=mesh, in_specs=in_specs, out_specs=out_specs, check_vma=False
    )
```

```python
import functools

import jax
import jax.numpy as jnp
from jax import lax
from jax.experimental import pallas as pl
from jax.experimental.pallas import tpu as pltpu
from jax.sharding import PartitionSpec as P

HEAD_DIM = 128
BLOCK = 512
EPSILON = 1e-06
AXES = ("seq", "head")
NZ, NX, NC, NY = 4, 4, 2, 4
OFFSETS = (0, 1, -1, 2)
QROWS = 256
CHUNKS = ((0, 128), (128, 128), (256, 256), (512, 256), (768, 256))
VMEM_LIMIT = 10 * 1024 * 1024
COST = pl.CostEstimate(flops=1, bytes_accessed=1, transcendentals=0)


def route(target):
    pairs = []
    for z in range(NZ):
        for x in range(NX):
            for c in range(NC):
                for y in range(NY):
                    z2, x2, c2, y2 = target(z, x, c, y)
                    source = ((z * NX + x) * NC + c) * NY + y
                    to = (((z2 % NZ) * NX + x2 % NX) * NC + c2) * NY + y2
                    pairs.append((source, to))
    return pairs


def send(array, target):
    return lax.ppermute(array, AXES, route(target))


def params():
    return pltpu.CompilerParams(vmem_limit_bytes=VMEM_LIMIT)


def feature(source):
    wide = source.astype(jnp.float32)
    return jnp.where(wide > 0, wide + 1.0, jnp.exp(jnp.minimum(wide, 0.0))).astype(jnp.bfloat16)


def state_kernel(keys_hbm, values_hbm, feat_ref, total_ref, first_ref, keys, values, arrived):
    groups, _, width = keys.shape
    copies = []
    for group in range(groups):
        columns = slice(group * width, (group + 1) * width)
        for index, (source, target) in enumerate(((keys_hbm, keys), (values_hbm, values))):
            copies.append(
                pltpu.make_async_copy(
                    source.at[:, columns], target.at[group], arrived.at[group, index]
                )
            )
            copies[-1].start()
    for group in range(groups):
        copies[2 * group].wait()
        copies[2 * group + 1].wait()
        for inner in range(width // HEAD_DIM):
            head = group * (width // HEAD_DIM) + inner
            here = slice(inner * HEAD_DIM, (inner + 1) * HEAD_DIM)
            feat = feature(keys[group, :, here])
            feat_ref[:, head * HEAD_DIM : (head + 1) * HEAD_DIM] = feat
            sums = []
            for block in range(2):
                rows = slice(block * BLOCK, (block + 1) * BLOCK)
                sums.append(
                    lax.dot_general(
                        feat[rows],
                        values[group, rows, here],
                        (((0,), (0,)), ((), ())),
                        preferred_element_type=jnp.float32,
                    )
                )
            first_ref[head] = sums[0]
            total_ref[head] = (sums[0] + sums[1]).astype(jnp.bfloat16)


def states(keys, values):
    tokens, features = keys.shape
    heads = features // HEAD_DIM
    groups = 4
    buffer = pltpu.VMEM((groups, tokens, features // groups), jnp.bfloat16)
    return pl.pallas_call(
        state_kernel,
        in_specs=[pl.BlockSpec(memory_space=pltpu.HBM)] * 2,
        out_shape=[
            jax.ShapeDtypeStruct((tokens, features), jnp.bfloat16),
            jax.ShapeDtypeStruct((heads, HEAD_DIM, HEAD_DIM), jnp.bfloat16),
            jax.ShapeDtypeStruct((heads, HEAD_DIM, HEAD_DIM), jnp.float32),
        ],
        scratch_shapes=[buffer, buffer, pltpu.SemaphoreType.DMA((groups, 2))],
        compiler_params=params(),
        cost_estimate=COST,
        name="states",
    )(keys, values)


def local_kernel(queries_ref, feat_ref, values_ref, local_ref, query_feat_ref):
    rows = queries_ref.shape[0]
    span = feat_ref.shape[0]
    row = lax.broadcasted_iota(jnp.int32, (rows, rows), 0)
    column = lax.broadcasted_iota(jnp.int32, (rows, rows), 1)
    causal = column <= row
    for head in range(queries_ref.shape[1] // HEAD_DIM):
        columns = slice(head * HEAD_DIM, (head + 1) * HEAD_DIM)
        query_feat = feature(queries_ref[:, columns])
        query_feat_ref[:, columns] = query_feat
        scores = lax.dot_general(
            query_feat,
            feat_ref[:, columns],
            (((1,), (1,)), ((), ())),
            preferred_element_type=jnp.float32,
        )
        diagonal = jnp.where(causal, scores[:, span - rows :], 0.0).astype(jnp.bfloat16)
        out = jnp.dot(
            diagonal, values_ref[span - rows :, columns], preferred_element_type=jnp.float32
        )
        if span > rows:
            out += jnp.dot(
                scores[:, : span - rows].astype(jnp.bfloat16),
                values_ref[: span - rows, columns],
                preferred_element_type=jnp.float32,
            )
        local_ref[:, columns] = out


def local_part(queries, key_feat, values, index):
    features = queries.shape[1]
    width = features // 2
    span = QROWS * (index % 2 + 1)
    first = (index // 2) * (BLOCK // span)
    rows = pl.BlockSpec((QROWS, width), lambda i: (index, i))
    source = pl.BlockSpec((span, width), lambda i: (first, i))
    out = pl.BlockSpec((QROWS, width), lambda i: (0, i))
    return pl.pallas_call(
        local_kernel,
        grid=(features // width,),
        in_specs=[rows, source, source],
        out_specs=[out, out],
        out_shape=[
            jax.ShapeDtypeStruct((QROWS, features), jnp.float32),
            jax.ShapeDtypeStruct((QROWS, features), jnp.bfloat16),
        ],
        compiler_params=params(),
        cost_estimate=COST,
        name="local_part",
    )(queries, key_feat, values)


def norm_kernel(local_ref, query_feat_ref, start_ref, normed_ref):
    for head in range(local_ref.shape[1] // HEAD_DIM):
        columns = slice(head * HEAD_DIM, (head + 1) * HEAD_DIM)
        combined = local_ref[:, columns] + jnp.dot(
            query_feat_ref[:, columns], start_ref[0, head], preferred_element_type=jnp.float32
        )
        mean = jnp.mean(combined * combined, axis=-1, keepdims=True)
        normed_ref[:, columns] = (combined * lax.rsqrt(mean + EPSILON)).astype(jnp.bfloat16)


def norm_part(local, query_feat, start, row, rows):
    features = local.shape[1]
    heads = features // HEAD_DIM
    block = row // BLOCK
    place = (row % QROWS) // rows
    spec = pl.BlockSpec((rows, features), lambda i: (place, 0))
    return pl.pallas_call(
        norm_kernel,
        grid=(1,),
        in_specs=[
            spec,
            spec,
            pl.BlockSpec((1, heads, HEAD_DIM, HEAD_DIM), lambda i: (block, 0, 0, 0)),
        ],
        out_specs=pl.BlockSpec((rows, features), lambda i: (0, 0)),
        out_shape=jax.ShapeDtypeStruct((rows, features), jnp.bfloat16),
        compiler_params=params(),
        cost_estimate=COST,
        name="norm_part",
    )(local, query_feat, start)


def position():
    seq = lax.axis_index("seq")
    return seq // (NX * NC), (seq // NC) % NX, seq % NC, lax.axis_index("head")


def after(value, *done):
    return lax.optimization_barrier((value, *done))[0]


def small(body, shapes, *operands, name):
    return pl.pallas_call(
        body,
        out_shape=shapes,
        compiler_params=params(),
        cost_estimate=COST,
        name=name,
    )(*operands)


def assemble_kernel(home, blocks, *refs):
    out_ref, arrived = refs[-2:]
    z, x, c, y = position()
    piece_rows, piece_columns = refs[0].shape[-2:]
    copies = []
    for number, (index, inner, place) in enumerate(blocks):
        from_z, from_x, core = place(z, x, c)
        kind = jnp.bitwise_xor(from_z, y)
        slot = jnp.where((kind == 0) | (kind == 3), 0, 1)
        second = jnp.where((kind < 2) == (home == 0), 0, 1)
        column = (from_x * NC + core) * piece_columns
        copies.append(
            pltpu.make_async_copy(
                refs[index].at[inner],
                out_ref.at[
                    slot,
                    pl.ds(pl.multiple_of(second * piece_rows, piece_rows), piece_rows),
                    pl.ds(pl.multiple_of(column, piece_columns), piece_columns),
                ],
                arrived.at[number],
            )
        )
    for copy in copies:
        copy.start()
    for copy in copies:
        copy.wait()


def assemble(home, blocks, *pieces):
    side = 2 * pieces[0].shape[-2]
    return pl.pallas_call(
        functools.partial(assemble_kernel, home, blocks),
        in_specs=[pl.BlockSpec(memory_space=pl.ANY)] * len(pieces),
        out_specs=pl.BlockSpec(memory_space=pl.ANY),
        out_shape=jax.ShapeDtypeStruct((2, side, side), jnp.bfloat16),
        scratch_shapes=[pltpu.SemaphoreType.DMA((len(blocks),))],
        compiler_params=params(),
        cost_estimate=COST,
        name="assemble",
    )(*pieces)


def product(normed_ref, peer_ref, weight_ref):
    total = jnp.dot(normed_ref[...], weight_ref[0], preferred_element_type=jnp.float32)
    return total + jnp.dot(peer_ref[...], weight_ref[1], preferred_element_type=jnp.float32)


def other_kernel(normed_ref, peer_ref, weight_ref, *out_refs):
    total = product(normed_ref, peer_ref, weight_ref).astype(jnp.bfloat16)
    rows = out_refs[0].shape[0]
    for index, out_ref in enumerate(out_refs):
        out_ref[...] = total[index * rows : (index + 1) * rows]


def project_other(normed, peer, weight, parts):
    rows, features = normed.shape
    out = jax.ShapeDtypeStruct((rows // parts, features), jnp.bfloat16)
    return pl.pallas_call(
        other_kernel,
        out_shape=[out] * parts,
        compiler_params=params(),
        cost_estimate=COST,
        name="project_other",
    )(normed, peer, weight)


def own_kernel(parts, normed_refs, peer_refs, weight_ref, received_refs, out_ref):
    row = 0
    received_refs = list(received_refs)
    for count, normed_ref, peer_ref in zip(parts, normed_refs, peer_refs):
        total = product(normed_ref, peer_ref, weight_ref)
        place = 0
        for _ in range(count):
            back_ref = received_refs.pop(0)
            rows = back_ref.shape[0]
            done = total[place : place + rows] + back_ref[...].astype(jnp.float32)
            out_ref[row : row + rows] = done.astype(jnp.bfloat16)
            place += rows
            row += rows


def project_own(normed, peers, weight, received, place, tokens, target):
    features = weight.shape[-1]
    rows = sum(chunk.shape[0] for chunk in normed)
    parts = [len(group) for group in received]
    flat = [part for group in received for part in group]
    count = len(normed)
    operands = [*normed, *peers, weight, *flat]
    specs = [pl.BlockSpec(array.shape, lambda i, n=array.ndim: (0,) * n) for array in operands]
    aliases = {}
    if target is not None:
        aliases = {len(operands): 0}
        operands.append(target)
        specs.append(pl.BlockSpec(memory_space=pl.ANY))

    def body(*refs):
        back = refs[2 * count + 1 : 2 * count + 1 + len(flat)]
        own_kernel(parts, refs[:count], refs[count : 2 * count], refs[2 * count], back, refs[-1])

    return pl.pallas_call(
        body,
        grid=(1,),
        in_specs=specs,
        out_specs=pl.BlockSpec((rows, features), lambda i: (place // rows, 0)),
        out_shape=jax.ShapeDtypeStruct((tokens, features), jnp.bfloat16),
        input_output_aliases=aliases,
        compiler_params=params(),
        cost_estimate=COST,
        name="project_own",
    )(*operands)


def early_kernel(normed_ref, peer_ref, weight_ref, out_ref):
    out_ref[...] = product(normed_ref, peer_ref, weight_ref)


def finish_kernel(early_ref, received_ref, _, out_ref):
    total = early_ref[...] + received_ref[...].astype(jnp.float32)
    out_ref[...] = total.astype(jnp.bfloat16)


def finish_last(early, received, place, target):
    rows, features = early.shape
    chunk = pl.BlockSpec((rows, features), lambda i: (0, 0))
    return pl.pallas_call(
        finish_kernel,
        grid=(1,),
        in_specs=[chunk, chunk, pl.BlockSpec(memory_space=pl.ANY)],
        out_specs=pl.BlockSpec((rows, features), lambda i: (place // rows, 0)),
        out_shape=jax.ShapeDtypeStruct(target.shape, target.dtype),
        input_output_aliases={2: 0},
        compiler_params=params(),
        cost_estimate=COST,
        name="finish_last",
    )(early, received, target)


def other_core(z, x, c, y):
    return z, x, 1 - c, y


def along_x(away, z, x, c, y):
    return z, x - away, c, y


def along_z(away, z, x, c, y):
    return z - away, x, c, y


def chip_kernel(total_ref, peer_ref, wide_ref, chip_ref):
    half = chip_ref.shape[0]
    mine = pl.ds(position()[2] * half, half)
    wide = total_ref[mine].astype(jnp.float32) + peer_ref[mine].astype(jnp.float32)
    wide_ref[...] = wide
    chip_ref[...] = wide.astype(jnp.bfloat16)


def step_kernel(axis, bit, *refs):
    wide_ref, other_ref, next_wide_ref, next_ref, earlier_out_ref = refs[0], *refs[-4:]
    place = position()[axis]
    other = other_ref[...].astype(jnp.float32)
    wide = wide_ref[...] + other
    earlier = jnp.where(jnp.bitwise_and(place, bit) != 0, other, 0.0)
    if len(refs) == 6:
        earlier += refs[1][...]
    next_wide_ref[...] = wide
    next_ref[...] = wide.astype(jnp.bfloat16)
    earlier_out_ref[...] = earlier


def last_kernel(earlier_ref, other_ref, half_ref):
    place = position()[0]
    other = other_ref[...].astype(jnp.float32)
    half_ref[...] = (earlier_ref[...] + jnp.where(place >= 2, other, 0.0)).astype(jnp.bfloat16)


def start_kernel(mine_ref, other_ref, peer_ref, first_ref, start_ref):
    core = position()[2]
    half = mine_ref.shape[0]
    for place in range(2):
        heads = slice(place * half, (place + 1) * half)
        carried = jnp.where(
            core == place, mine_ref[...].astype(jnp.float32), other_ref[...].astype(jnp.float32)
        )
        carried += jnp.where(core == 1, peer_ref[heads].astype(jnp.float32), 0.0)
        start_ref[0, heads] = carried.astype(jnp.bfloat16)
        start_ref[1, heads] = (carried + first_ref[heads]).astype(jnp.bfloat16)


def home(z, y):
    return (z, y) if (z ^ y) in (0, 3) else (z ^ 1, y ^ 1)


def item_kernel(a_ref, b_ref, own_ref, other_ref):
    z, _, _, y = position()
    far = jnp.bitwise_xor(z, y) >= 2
    own_ref[...] = jnp.where(far, b_ref[...], a_ref[...])
    other_ref[...] = jnp.where(far, a_ref[...], b_ref[...])


def spread_weight(weight):
    rows = weight.shape[0] // 2

    def to(second, z, x, c, y):
        z, y = home(z, y)
        return (z ^ 3 if second else z), x, c, y

    parts = [weight[:rows], weight[rows:]]
    return parts[0], [send(part, functools.partial(to, i)) for i, part in enumerate(parts)]


def first_moves(item):
    return [item] + [send(item, functools.partial(line_move, True, away)) for away in OFFSETS[1:]]


def paced_moves(item, first):
    near = [send(item, functools.partial(line_move, first, away)) for away in OFFSETS[1:3]]
    far = send(after(item, *near), functools.partial(line_move, first, OFFSETS[3]))
    return [item, *near, far]


def second_moves(line):
    return [line] + [send(line, functools.partial(line_move, False, away)) for away in OFFSETS[1:]]


def line_move(first, away, z, x, c, y):
    return along_x(away, z, x, c, y) if (c == 0) == first else along_z(away, z, x, c, y)


def line_place(mine, outer, inner, z, x, c):
    core = c if mine else 1 - c
    from_z = lax.rem(z + jnp.where(core == 0, outer, inner) + NZ, NZ)
    from_x = lax.rem(x + jnp.where(core == 0, inner, outer) + NX, NX)
    return from_z, from_x, core


def pair_place(mine, outer, inner, z, x, c):
    from_z, from_x, core = line_place(True, outer, inner, z, x, c)
    return from_z, from_x, core if mine else 1 - core


PAIR_BLOCKS = [
    (index, (inner, side), functools.partial(pair_place, side == 0, OFFSETS[index], OFFSETS[inner]))
    for index in range(4)
    for inner in range(4)
    for side in range(2)
]

LINE_BLOCKS = [
    (index, inner, functools.partial(line_place, index < 4, OFFSETS[index % 4], OFFSETS[inner]))
    for index in range(8)
    for inner in range(4)
]


def on_device(queries, keys, values, out_weight):
    tokens = queries.shape[0]

    key_feat, total, first = states(keys, values)
    _, parts = spread_weight(after(out_weight, total))
    heads = total.shape[0]
    half = jax.ShapeDtypeStruct((heads // 2, HEAD_DIM, HEAD_DIM), jnp.bfloat16)
    wide_half = jax.ShapeDtypeStruct(half.shape, jnp.float32)

    peer = send(total, other_core)
    wide, chip = small(chip_kernel, [wide_half, half], total, peer, name="chip_sum")
    other_chip = send(chip, lambda z, x, c, y: (z, x ^ 1, c, y))
    local = [local_part(after(queries, chip), key_feat, values, 0)]
    wide, chip, earlier = small(
        functools.partial(step_kernel, 1, 1),
        [wide_half, half, wide_half],
        wide,
        after(other_chip, local[0][0]),
        name="step_x",
    )
    other_chip = send(chip, lambda z, x, c, y: (z, 3 - x, c, y))
    item = jax.ShapeDtypeStruct(parts[0].shape, parts[0].dtype)
    own_item, other_item = small(
        item_kernel, [item, item], *after(tuple(parts), chip), name="weight_items"
    )
    line = first_moves(other_item)
    other_chip = after(other_chip, other_item)
    wide, chip, earlier = small(
        functools.partial(step_kernel, 1, 2),
        [wide_half, half, wide_half],
        wide,
        earlier,
        other_chip,
        name="step_x2",
    )
    other_chip = send(chip, lambda z, x, c, y: (z ^ 1, x, c, y))
    wide, chip, earlier = small(
        functools.partial(step_kernel, 0, 1),
        [wide_half, half, wide_half],
        wide,
        earlier,
        other_chip,
        name="step_z",
    )
    other_chip = send(chip, lambda z, x, c, y: (3 - z, x, c, y))
    line = jnp.stack(after(tuple(line), chip))
    lines = second_moves(line)
    my_half = small(last_kernel, half, earlier, after(other_chip, line), name="step_z2")
    other_half = send(my_half, other_core)
    start = small(
        start_kernel,
        jax.ShapeDtypeStruct((2, heads, HEAD_DIM, HEAD_DIM), jnp.bfloat16),
        my_half,
        other_half,
        peer,
        first,
        name="start_states",
    )

    normed, peers, partial, received = [], [], [], []
    parts = (1, 1, 1, 1, 1)

    def norm(index, *done):
        place, rows = CHUNKS[index]
        number = place // QROWS
        if number == len(local):
            local.append(local_part(after(queries, *done), key_feat, values, number))
        query_feat = after(local[number][1], *done) if done else local[number][1]
        normed.append(norm_part(local[number][0], query_feat, start, place, rows))
        ready = after(normed[-1], peers[1]) if index == 2 else normed[-1]
        peers.append(send(ready, lambda z, x, c, y: (z, x, c, y ^ 1)))

    def other(index, *done):
        if done:
            peers[index] = after(peers[index], *done)
        partial.append(project_other(normed[index], peers[index], weight, parts[index]))
        received.append(
            [send(part, lambda z, x, c, y: (z, x, c, 3 - y)) for part in partial[index]]
        )

    norm(0)
    norm(1, normed[0])
    norm(2, normed[1])
    norm(3, normed[2])
    lines = list(after(tuple(lines), peers[0], normed[3]))
    swapped = [send(piece, other_core) for piece in lines]
    weight = assemble(1, LINE_BLOCKS, *lines, *swapped)
    other(0)
    norm(4, partial[0][0])
    other(1, normed[4])
    own_pair = jnp.stack([own_item, send(after(own_item, partial[1][0]), other_core)])
    own_line = first_moves(own_pair)
    other(2, received[0][0], normed[4])
    own_lines = second_moves(jnp.stack(after(tuple(own_line), partial[2][0], received[1][0])))
    other(3, partial[2][0], received[1][0], received[2][0])
    other(4, partial[3][0])
    own_weight = assemble(0, PAIR_BLOCKS, *after(tuple(own_lines), partial[4][0]))
    out = project_own(normed[:4], peers[:4], own_weight, received[:4], 0, tokens, None)
    early = small(
        early_kernel,
        jax.ShapeDtypeStruct(normed[4].shape, jnp.float32),
        normed[4],
        after(peers[4], out),
        own_weight,
        name="early_product",
    )
    back = after(received[4][0], early)
    return finish_last(early, back, CHUNKS[4][0], out)


def solution(mesh):
    in_specs = (P("seq", "head"), P("seq", "head"), P("seq", "head"), P("head", "seq"))
    out_specs = P("seq", "head")
    return jax.shard_map(
        on_device, mesh=mesh, in_specs=in_specs, out_specs=out_specs, check_vma=False
    )
```

```python
import functools

import jax
import jax.numpy as jnp
from jax import lax
from jax.experimental import pallas as pl
from jax.experimental.pallas import tpu as pltpu
from jax.sharding import PartitionSpec as P

HEAD_DIM = 128
BLOCK = 512
EPSILON = 1e-06
AXES = ("seq", "head")
NZ, NX, NC, NY = 4, 4, 2, 4
OFFSETS = (0, 1, -1, 2)
QROWS = 256
CHUNKS = ((0, 128), (128, 128), (256, 256), (512, 256), (768, 256))
VMEM_LIMIT = 10 * 1024 * 1024
COST = pl.CostEstimate(flops=1, bytes_accessed=1, transcendentals=0)


def route(target):
    pairs = []
    for z in range(NZ):
        for x in range(NX):
            for c in range(NC):
                for y in range(NY):
                    z2, x2, c2, y2 = target(z, x, c, y)
                    source = ((z * NX + x) * NC + c) * NY + y
                    to = (((z2 % NZ) * NX + x2 % NX) * NC + c2) * NY + y2
                    pairs.append((source, to))
    return pairs


def send(array, target):
    return lax.ppermute(array, AXES, route(target))


def params():
    return pltpu.CompilerParams(vmem_limit_bytes=VMEM_LIMIT)


def feature(source):
    wide = source.astype(jnp.float32)
    return jnp.where(wide > 0, wide + 1.0, jnp.exp(jnp.minimum(wide, 0.0))).astype(jnp.bfloat16)


def state_kernel(keys_hbm, values_hbm, feat_ref, total_ref, first_ref, keys, values, arrived):
    groups, _, width = keys.shape
    copies = []
    for group in range(groups):
        columns = slice(group * width, (group + 1) * width)
        for index, (source, target) in enumerate(((keys_hbm, keys), (values_hbm, values))):
            copies.append(
                pltpu.make_async_copy(
                    source.at[:, columns], target.at[group], arrived.at[group, index]
                )
            )
            copies[-1].start()
    for group in range(groups):
        copies[2 * group].wait()
        copies[2 * group + 1].wait()
        for inner in range(width // HEAD_DIM):
            head = group * (width // HEAD_DIM) + inner
            here = slice(inner * HEAD_DIM, (inner + 1) * HEAD_DIM)
            feat = feature(keys[group, :, here])
            feat_ref[:, head * HEAD_DIM : (head + 1) * HEAD_DIM] = feat
            sums = []
            for block in range(2):
                rows = slice(block * BLOCK, (block + 1) * BLOCK)
                sums.append(
                    lax.dot_general(
                        feat[rows],
                        values[group, rows, here],
                        (((0,), (0,)), ((), ())),
                        preferred_element_type=jnp.float32,
                    )
                )
            first_ref[head] = sums[0]
            total_ref[head] = (sums[0] + sums[1]).astype(jnp.bfloat16)


def states(keys, values):
    tokens, features = keys.shape
    heads = features // HEAD_DIM
    groups = 4
    buffer = pltpu.VMEM((groups, tokens, features // groups), jnp.bfloat16)
    return pl.pallas_call(
        state_kernel,
        in_specs=[pl.BlockSpec(memory_space=pltpu.HBM)] * 2,
        out_shape=[
            jax.ShapeDtypeStruct((tokens, features), jnp.bfloat16),
            jax.ShapeDtypeStruct((heads, HEAD_DIM, HEAD_DIM), jnp.bfloat16),
            jax.ShapeDtypeStruct((heads, HEAD_DIM, HEAD_DIM), jnp.float32),
        ],
        scratch_shapes=[buffer, buffer, pltpu.SemaphoreType.DMA((groups, 2))],
        compiler_params=params(),
        cost_estimate=COST,
        name="states",
    )(keys, values)


def local_kernel(queries_ref, feat_ref, values_ref, local_ref, query_feat_ref):
    rows = queries_ref.shape[0]
    span = feat_ref.shape[0]
    row = lax.broadcasted_iota(jnp.int32, (rows, rows), 0)
    column = lax.broadcasted_iota(jnp.int32, (rows, rows), 1)
    causal = column <= row
    for head in range(queries_ref.shape[1] // HEAD_DIM):
        columns = slice(head * HEAD_DIM, (head + 1) * HEAD_DIM)
        query_feat = feature(queries_ref[:, columns])
        query_feat_ref[:, columns] = query_feat
        scores = lax.dot_general(
            query_feat,
            feat_ref[:, columns],
            (((1,), (1,)), ((), ())),
            preferred_element_type=jnp.float32,
        )
        diagonal = jnp.where(causal, scores[:, span - rows :], 0.0).astype(jnp.bfloat16)
        out = jnp.dot(
            diagonal, values_ref[span - rows :, columns], preferred_element_type=jnp.float32
        )
        if span > rows:
            out += jnp.dot(
                scores[:, : span - rows].astype(jnp.bfloat16),
                values_ref[: span - rows, columns],
                preferred_element_type=jnp.float32,
            )
        local_ref[:, columns] = out


def local_part(queries, key_feat, values, index):
    features = queries.shape[1]
    width = features // 2
    span = QROWS * (index % 2 + 1)
    first = (index // 2) * (BLOCK // span)
    rows = pl.BlockSpec((QROWS, width), lambda i: (index, i))
    source = pl.BlockSpec((span, width), lambda i: (first, i))
    out = pl.BlockSpec((QROWS, width), lambda i: (0, i))
    return pl.pallas_call(
        local_kernel,
        grid=(features // width,),
        in_specs=[rows, source, source],
        out_specs=[out, out],
        out_shape=[
            jax.ShapeDtypeStruct((QROWS, features), jnp.float32),
            jax.ShapeDtypeStruct((QROWS, features), jnp.bfloat16),
        ],
        compiler_params=params(),
        cost_estimate=COST,
        name="local_part",
    )(queries, key_feat, values)


def norm_kernel(local_ref, query_feat_ref, start_ref, normed_ref):
    for head in range(local_ref.shape[1] // HEAD_DIM):
        columns = slice(head * HEAD_DIM, (head + 1) * HEAD_DIM)
        combined = local_ref[:, columns] + jnp.dot(
            query_feat_ref[:, columns], start_ref[0, head], preferred_element_type=jnp.float32
        )
        mean = jnp.mean(combined * combined, axis=-1, keepdims=True)
        normed_ref[:, columns] = (combined * lax.rsqrt(mean + EPSILON)).astype(jnp.bfloat16)


def norm_part(local, query_feat, start, row, rows):
    features = local.shape[1]
    heads = features // HEAD_DIM
    block = row // BLOCK
    place = (row % QROWS) // rows
    spec = pl.BlockSpec((rows, features), lambda i: (place, 0))
    return pl.pallas_call(
        norm_kernel,
        grid=(1,),
        in_specs=[
            spec,
            spec,
            pl.BlockSpec((1, heads, HEAD_DIM, HEAD_DIM), lambda i: (block, 0, 0, 0)),
        ],
        out_specs=pl.BlockSpec((rows, features), lambda i: (0, 0)),
        out_shape=jax.ShapeDtypeStruct((rows, features), jnp.bfloat16),
        compiler_params=params(),
        cost_estimate=COST,
        name="norm_part",
    )(local, query_feat, start)


def position():
    seq = lax.axis_index("seq")
    return seq // (NX * NC), (seq // NC) % NX, seq % NC, lax.axis_index("head")


def after(value, *done):
    return lax.optimization_barrier((value, *done))[0]


def small(body, shapes, *operands, name):
    return pl.pallas_call(
        body,
        out_shape=shapes,
        compiler_params=params(),
        cost_estimate=COST,
        name=name,
    )(*operands)


def assemble_kernel(home, blocks, *refs):
    out_ref, arrived = refs[-2:]
    z, x, c, y = position()
    piece_rows, piece_columns = refs[0].shape[-2:]
    copies = []
    for number, (index, inner, place) in enumerate(blocks):
        from_z, from_x, core = place(z, x, c)
        kind = jnp.bitwise_xor(from_z, y)
        slot = jnp.where((kind == 0) | (kind == 3), 0, 1)
        second = jnp.where((kind < 2) == (home == 0), 0, 1)
        column = (from_x * NC + core) * piece_columns
        copies.append(
            pltpu.make_async_copy(
                refs[index].at[inner],
                out_ref.at[
                    slot,
                    pl.ds(pl.multiple_of(second * piece_rows, piece_rows), piece_rows),
                    pl.ds(pl.multiple_of(column, piece_columns), piece_columns),
                ],
                arrived.at[number],
            )
        )
    for copy in copies:
        copy.start()
    for copy in copies:
        copy.wait()


def assemble(home, blocks, *pieces):
    side = 2 * pieces[0].shape[-2]
    return pl.pallas_call(
        functools.partial(assemble_kernel, home, blocks),
        in_specs=[pl.BlockSpec(memory_space=pl.ANY)] * len(pieces),
        out_specs=pl.BlockSpec(memory_space=pl.ANY),
        out_shape=jax.ShapeDtypeStruct((2, side, side), jnp.bfloat16),
        scratch_shapes=[pltpu.SemaphoreType.DMA((len(blocks),))],
        compiler_params=params(),
        cost_estimate=COST,
        name="assemble",
    )(*pieces)


def product(normed_ref, peer_ref, weight_ref):
    total = jnp.dot(normed_ref[...], weight_ref[0], preferred_element_type=jnp.float32)
    return total + jnp.dot(peer_ref[...], weight_ref[1], preferred_element_type=jnp.float32)


def other_kernel(normed_ref, peer_ref, weight_ref, *out_refs):
    total = product(normed_ref, peer_ref, weight_ref).astype(jnp.bfloat16)
    rows = out_refs[0].shape[0]
    for index, out_ref in enumerate(out_refs):
        out_ref[...] = total[index * rows : (index + 1) * rows]


def project_other(normed, peer, weight, parts):
    rows, features = normed.shape
    out = jax.ShapeDtypeStruct((rows // parts, features), jnp.bfloat16)
    return pl.pallas_call(
        other_kernel,
        out_shape=[out] * parts,
        compiler_params=params(),
        cost_estimate=COST,
        name="project_other",
    )(normed, peer, weight)


def own_kernel(parts, normed_refs, peer_refs, weight_ref, received_refs, out_ref):
    row = 0
    received_refs = list(received_refs)
    for count, normed_ref, peer_ref in zip(parts, normed_refs, peer_refs):
        total = product(normed_ref, peer_ref, weight_ref)
        place = 0
        for _ in range(count):
            back_ref = received_refs.pop(0)
            rows = back_ref.shape[0]
            done = total[place : place + rows] + back_ref[...].astype(jnp.float32)
            out_ref[row : row + rows] = done.astype(jnp.bfloat16)
            place += rows
            row += rows


def project_own(normed, peers, weight, received, place, tokens, target):
    features = weight.shape[-1]
    rows = sum(chunk.shape[0] for chunk in normed)
    parts = [len(group) for group in received]
    flat = [part for group in received for part in group]
    count = len(normed)
    operands = [*normed, *peers, weight, *flat]
    specs = [pl.BlockSpec(array.shape, lambda i, n=array.ndim: (0,) * n) for array in operands]
    aliases = {}
    if target is not None:
        aliases = {len(operands): 0}
        operands.append(target)
        specs.append(pl.BlockSpec(memory_space=pl.ANY))

    def body(*refs):
        back = refs[2 * count + 1 : 2 * count + 1 + len(flat)]
        own_kernel(parts, refs[:count], refs[count : 2 * count], refs[2 * count], back, refs[-1])

    return pl.pallas_call(
        body,
        grid=(1,),
        in_specs=specs,
        out_specs=pl.BlockSpec((rows, features), lambda i: (place // rows, 0)),
        out_shape=jax.ShapeDtypeStruct((tokens, features), jnp.bfloat16),
        input_output_aliases=aliases,
        compiler_params=params(),
        cost_estimate=COST,
        name="project_own",
    )(*operands)


def other_core(z, x, c, y):
    return z, x, 1 - c, y


def along_x(away, z, x, c, y):
    return z, x - away, c, y


def along_z(away, z, x, c, y):
    return z - away, x, c, y


def chip_kernel(total_ref, peer_ref, wide_ref, chip_ref):
    half = chip_ref.shape[0]
    mine = pl.ds(position()[2] * half, half)
    wide = total_ref[mine].astype(jnp.float32) + peer_ref[mine].astype(jnp.float32)
    wide_ref[...] = wide
    chip_ref[...] = wide.astype(jnp.bfloat16)


def step_kernel(axis, bit, *refs):
    wide_ref, other_ref, next_wide_ref, next_ref, earlier_out_ref = refs[0], *refs[-4:]
    place = position()[axis]
    other = other_ref[...].astype(jnp.float32)
    wide = wide_ref[...] + other
    earlier = jnp.where(jnp.bitwise_and(place, bit) != 0, other, 0.0)
    if len(refs) == 6:
        earlier += refs[1][...]
    next_wide_ref[...] = wide
    next_ref[...] = wide.astype(jnp.bfloat16)
    earlier_out_ref[...] = earlier


def last_kernel(earlier_ref, other_ref, half_ref):
    place = position()[0]
    other = other_ref[...].astype(jnp.float32)
    half_ref[...] = (earlier_ref[...] + jnp.where(place >= 2, other, 0.0)).astype(jnp.bfloat16)


def start_kernel(mine_ref, other_ref, peer_ref, first_ref, start_ref):
    core = position()[2]
    half = mine_ref.shape[0]
    for place in range(2):
        heads = slice(place * half, (place + 1) * half)
        carried = jnp.where(
            core == place, mine_ref[...].astype(jnp.float32), other_ref[...].astype(jnp.float32)
        )
        carried += jnp.where(core == 1, peer_ref[heads].astype(jnp.float32), 0.0)
        start_ref[0, heads] = carried.astype(jnp.bfloat16)
        start_ref[1, heads] = (carried + first_ref[heads]).astype(jnp.bfloat16)


def home(z, y):
    return (z, y) if (z ^ y) in (0, 3) else (z ^ 1, y ^ 1)


def item_kernel(a_ref, b_ref, own_ref, other_ref):
    z, _, _, y = position()
    far = jnp.bitwise_xor(z, y) >= 2
    own_ref[...] = jnp.where(far, b_ref[...], a_ref[...])
    other_ref[...] = jnp.where(far, a_ref[...], b_ref[...])


def spread_weight(weight):
    rows = weight.shape[0] // 2

    def to(second, z, x, c, y):
        z, y = home(z, y)
        return (z ^ 3 if second else z), x, c, y

    parts = [weight[:rows], weight[rows:]]
    return parts[0], [send(part, functools.partial(to, i)) for i, part in enumerate(parts)]


def first_moves(item):
    return [item] + [send(item, functools.partial(line_move, True, away)) for away in OFFSETS[1:]]


def paced_moves(item, first):
    near = [send(item, functools.partial(line_move, first, away)) for away in OFFSETS[1:3]]
    far = send(after(item, *near), functools.partial(line_move, first, OFFSETS[3]))
    return [item, *near, far]


def second_moves(line):
    return [line] + [send(line, functools.partial(line_move, False, away)) for away in OFFSETS[1:]]


def line_move(first, away, z, x, c, y):
    return along_x(away, z, x, c, y) if (c == 0) == first else along_z(away, z, x, c, y)


def line_place(mine, outer, inner, z, x, c):
    core = c if mine else 1 - c
    from_z = lax.rem(z + jnp.where(core == 0, outer, inner) + NZ, NZ)
    from_x = lax.rem(x + jnp.where(core == 0, inner, outer) + NX, NX)
    return from_z, from_x, core


def pair_place(mine, outer, inner, z, x, c):
    from_z, from_x, core = line_place(True, outer, inner, z, x, c)
    return from_z, from_x, core if mine else 1 - core


PAIR_BLOCKS = [
    (index, (inner, side), functools.partial(pair_place, side == 0, OFFSETS[index], OFFSETS[inner]))
    for index in range(4)
    for inner in range(4)
    for side in range(2)
]

LINE_BLOCKS = [
    (index, inner, functools.partial(line_place, index < 4, OFFSETS[index % 4], OFFSETS[inner]))
    for index in range(8)
    for inner in range(4)
]


def on_device(queries, keys, values, out_weight):
    tokens = queries.shape[0]

    key_feat, total, first = states(keys, values)
    _, parts = spread_weight(after(out_weight, total))
    heads = total.shape[0]
    half = jax.ShapeDtypeStruct((heads // 2, HEAD_DIM, HEAD_DIM), jnp.bfloat16)
    wide_half = jax.ShapeDtypeStruct(half.shape, jnp.float32)

    peer = send(total, other_core)
    wide, chip = small(chip_kernel, [wide_half, half], total, peer, name="chip_sum")
    other_chip = send(chip, lambda z, x, c, y: (z, x ^ 1, c, y))
    local = [local_part(after(queries, chip), key_feat, values, 0)]
    wide, chip, earlier = small(
        functools.partial(step_kernel, 1, 1),
        [wide_half, half, wide_half],
        wide,
        after(other_chip, local[0][0]),
        name="step_x",
    )
    other_chip = send(chip, lambda z, x, c, y: (z, 3 - x, c, y))
    item = jax.ShapeDtypeStruct(parts[0].shape, parts[0].dtype)
    own_item, other_item = small(
        item_kernel, [item, item], *after(tuple(parts), chip), name="weight_items"
    )
    line = first_moves(other_item)
    other_chip = after(other_chip, other_item)
    wide, chip, earlier = small(
        functools.partial(step_kernel, 1, 2),
        [wide_half, half, wide_half],
        wide,
        earlier,
        other_chip,
        name="step_x2",
    )
    other_chip = send(chip, lambda z, x, c, y: (z ^ 1, x, c, y))
    wide, chip, earlier = small(
        functools.partial(step_kernel, 0, 1),
        [wide_half, half, wide_half],
        wide,
        earlier,
        other_chip,
        name="step_z",
    )
    other_chip = send(chip, lambda z, x, c, y: (3 - z, x, c, y))
    line = jnp.stack(after(tuple(line), chip))
    lines = second_moves(line)
    my_half = small(last_kernel, half, earlier, after(other_chip, line), name="step_z2")
    other_half = send(my_half, other_core)
    start = small(
        start_kernel,
        jax.ShapeDtypeStruct((2, heads, HEAD_DIM, HEAD_DIM), jnp.bfloat16),
        my_half,
        other_half,
        peer,
        first,
        name="start_states",
    )

    normed, peers, partial, received = [], [], [], []
    parts = (1, 1, 1, 1, 1)

    def norm(index, *done):
        place, rows = CHUNKS[index]
        number = place // QROWS
        if number == len(local):
            local.append(local_part(after(queries, *done), key_feat, values, number))
        query_feat = after(local[number][1], *done) if done else local[number][1]
        normed.append(norm_part(local[number][0], query_feat, start, place, rows))
        ready = after(normed[-1], peers[1]) if index == 2 else normed[-1]
        peers.append(send(ready, lambda z, x, c, y: (z, x, c, y ^ 1)))

    def other(index, *done):
        if done:
            peers[index] = after(peers[index], *done)
        partial.append(project_other(normed[index], peers[index], weight, parts[index]))
        received.append(
            [send(part, lambda z, x, c, y: (z, x, c, 3 - y)) for part in partial[index]]
        )

    norm(0)
    norm(1, normed[0])
    norm(2, normed[1])
    norm(3, normed[2])
    lines = list(after(tuple(lines), peers[0], normed[3]))
    swapped = [send(piece, other_core) for piece in lines]
    weight = assemble(1, LINE_BLOCKS, *lines, *swapped)
    other(0)
    norm(4, partial[0][0])
    other(1, normed[4])
    own_pair = jnp.stack([own_item, send(after(own_item, partial[1][0], received[0][0]), other_core)])
    own_line = first_moves(own_pair)
    other(2, received[0][0], normed[4])
    own_lines = second_moves(jnp.stack(after(tuple(own_line), partial[2][0], received[1][0])))
    other(3, partial[2][0], received[1][0], received[2][0])
    other(4, partial[3][0])
    own_weight = assemble(0, PAIR_BLOCKS, *after(tuple(own_lines), partial[4][0]))
    out = project_own(normed[:4], peers[:4], own_weight, received[:4], 0, tokens, None)
    return project_own(
        normed[4:], peers[4:], own_weight, received[4:], CHUNKS[4][0], tokens, out
    )


def solution(mesh):
    in_specs = (P("seq", "head"), P("seq", "head"), P("seq", "head"), P("head", "seq"))
    out_specs = P("seq", "head")
    return jax.shard_map(
        on_device, mesh=mesh, in_specs=in_specs, out_specs=out_specs, check_vma=False
    )
```
